32 devices in a mesh: rep: 4 (over y, x), fsdp: 8 (over z, core).
Axes of the slice: x: 2, y: 2, z: 4, core: 2. Of those that a mesh axis runs over, the one named last changes fastest.
Arguments:
- gate_pre: bfloat16 [2048, 12288], P('rep', 'fsdp'), may hold values from -6 to 6
- up_pre: bfloat16 [2048, 12288], P('rep', 'fsdp'), may hold values from -40 to 40
- out_grad: bfloat16 [2048, 3072], P('rep'), may hold values from -6 to 6
- inner_params: bfloat16 [4, 12288, 3072], P('rep', 'fsdp'), may hold values from -0.109375 to 0.109375
- global_params: float32 [12288, 3072], P('fsdp', 'rep'), may hold values from -0.109375 to 0.109375
- outer_momentum: float32 [12288, 3072], P('fsdp', 'rep'), may hold values from -0.15625 to 0.15625
- pair_codes: int32 [4, 12288, 1536], P('rep', 'fsdp'), may hold values from 0 to 255
- code_scales: float32 [4, 12288, 24], P('rep', 'fsdp'), may hold values from 0.001 to 0.01
Outputs:
- merged_params: bfloat16 [4, 12288, 3072], P('rep', 'fsdp')
- new_global: float32 [12288, 3072], P('fsdp', 'rep')
- new_momentum: float32 [12288, 3072], P('fsdp', 'rep')
The draws below stay inside these ranges and needn't reach their ends.
Inputs may be any that keep to these rules, and one draw needn't show every extreme that they name: `pair_codes`: each word holds two codes of 0 to 15: its value mod 16 for column 2 j and its value // 16 for column 2 j + 1.
All inputs are finite; a program needn't handle non-finite values.
Results may differ from the reference program's by a relative error of at most 0.011.
Values may be sent and summed in bfloat16 or wider, within the bound.
A program may use at most 128 MiB of HBM per device.

```python
import math
import jax
import jax.numpy as jnp
from jax import lax

D = 3072
UNITS = 12288
BLOCK = 128
TOK_REP = 512
TOKENS = 2048
N_REP = 4


def draw_up_pre(key, part):
    key = jax.random.fold_in(key, 5)
    base_key, rough_key = jax.random.split(key)
    column = jnp.arange(UNITS, dtype=jnp.float32) / UNITS
    rough = jnp.exp(jax.random.uniform(rough_key, (UNITS,), jnp.float32, 0.0, 0.7))
    base = jnp.clip(jax.random.normal(base_key, (TOKENS, UNITS), jnp.float32), -6.0, 6.0)
    rising = 10.0 ** (column - 0.5)
    return (base * (rising * rough)[None, :]).astype(jnp.bfloat16)


def plant(array, own_key, least, top_value):
    longest = array.shape.index(max(array.shape))
    spots = []
    for shift in (0, 1):
        where = [jax.random.randint(jax.random.fold_in(own_key, axis), (), 0, length) for axis, length in enumerate(array.shape)]
        where[longest] = (where[longest] + shift) % array.shape[longest]
        spots.append(tuple(where))
    return array.at[spots[0]].set(least).at[spots[1]].set(top_value)


def shard_levels(key, dims, shards, smallest, top_value):
    factor_of, own = 1.0, jax.random.fold_in(key, 6)
    for axis_at, shards_of in shards:
        steps = jnp.exp(jax.random.uniform(jax.random.fold_in(own, axis_at), (shards_of,), jnp.float32, smallest / len(shards), top_value / len(shards)))
        factor_of = factor_of * jnp.repeat(steps, dims[axis_at] // shards_of).reshape([-1 if axis == axis_at else 1 for axis in range(len(dims))])
    return factor_of


def gaussian(rng, extent, deviation, bound, pieces=(), held_as=jnp.bfloat16):
    array = jax.random.normal(rng, extent, jnp.float32) * deviation
    if len(pieces) > 0:
        array = shard_levels(rng, extent, pieces, -0.22, 0.18) * array
    return jnp.clip(array, min=-bound, max=bound).astype(held_as)


def setup_inputs(seed: int = 0) -> dict:
    splits = jax.random.split(jax.random.key(seed), 9)
    gate_pre = gaussian(splits[0], (TOKENS, UNITS), 1.0, 6.0, ((0, 4), (1, 8)))
    up_pre = draw_up_pre(jax.random.fold_in(splits[8], 71), 0)
    out_grad = gaussian(splits[2], (TOKENS, D), 1.0, 6.0, ((0, 4),))
    inner_params = gaussian(splits[3], (N_REP, UNITS, D), D ** -0.5, 0.109375, ((0, 4), (1, 8)))
    global_params = gaussian(splits[4], (UNITS, D), D ** -0.5, 0.109375, ((0, 8), (1, 4)), jnp.float32)
    outer_momentum = gaussian(splits[5], (UNITS, D), 0.01, 0.15625, ((0, 8), (1, 4)), jnp.float32)
    pair_codes = plant(jax.random.randint(splits[6], (N_REP, UNITS, D // 2), 0, 256), jax.random.fold_in(splits[6], 1), 0, 255).astype(jnp.int32)
    code_scales = jnp.clip(jnp.exp(math.log(0.01) - 2.30258502 * jax.random.uniform(splits[7], (N_REP, UNITS, D // BLOCK), jnp.float32) ** shard_levels(splits[7], (N_REP, UNITS, D // BLOCK), ((0, 4), (1, 8)), -0.2, 0.2)), 0.001, 0.01)
    return dict(gate_pre=gate_pre, up_pre=up_pre, out_grad=out_grad, inner_params=inner_params, global_params=global_params, outer_momentum=outer_momentum, pair_codes=pair_codes, code_scales=code_scales)


def unpack(packed, scales):
    lower_code = packed % 16
    upper_code = packed // 16
    unpacked = jnp.stack([lower_code, upper_code], axis=-1).reshape(packed.shape[:-1] + (2 * packed.shape[-1],))
    centered = (unpacked - 8).astype(jnp.float32)
    blocks = centered.reshape(packed.shape[:-1] + (scales.shape[-1], -1)) * scales[..., None]
    return blocks.reshape(unpacked.shape).astype(jnp.bfloat16)

def reference(gate_pre, up_pre, out_grad, inner_params, global_params, outer_momentum, pair_codes, code_scales):

    def add_replica(running, item_pair):
        return (running + unpack(item_pair[0], item_pair[1]).astype(jnp.float32), None)
    running, _ = lax.scan(add_replica, jnp.zeros((UNITS, D), jnp.float32), (pair_codes, code_scales))
    mean_delta = running * (1.0 / N_REP)
    new_momentum = 0.9 * outer_momentum + mean_delta
    new_global = global_params - 0.7 * (mean_delta + 0.9 * new_momentum)
    global_bf = lax.optimization_barrier(new_global.astype(jnp.bfloat16)).astype(jnp.float32)
    gate_f32 = gate_pre.astype(jnp.float32)
    upper = up_pre.astype(jnp.float32)
    sigmoid_gate = jax.nn.sigmoid(gate_f32)
    hidden = (gate_f32 * sigmoid_gate * upper).astype(jnp.bfloat16)
    hidden_rows = hidden.reshape(N_REP, TOK_REP, UNITS)
    grad_rows = out_grad.reshape(N_REP, TOK_REP, D)

    def one_replica(replica_items):
        hidden_part, grad_part, params = replica_items
        grads = jnp.dot(hidden_part.T, grad_part, preferred_element_type=jnp.float32) * (1.0 / TOK_REP)
        root_mean = jnp.sqrt(jnp.sum(grads * grads) / (UNITS * D) + 1e-06)
        clipped = grads * jnp.minimum(1.0, 0.02 / root_mean)
        master = params.astype(jnp.float32)
        stepped = master - 0.8 * (clipped + 0.2 * master)
        return (0.5 * stepped + 0.5 * global_bf).astype(jnp.bfloat16)
    merged_params = lax.map(one_replica, (hidden_rows, grad_rows, inner_params))
    return (merged_params, new_global, new_momentum)
```

```python
import functools
import jax
import jax.numpy as jnp
from jax import lax
from jax.experimental import pallas as pl
from jax.experimental.pallas import tpu as pltpu
from jax.sharding import PartitionSpec as P


def outer_update(mean_delta, momentum, params):
    new_momentum = 0.9 * momentum + mean_delta
    new_global = params - 0.7 * (mean_delta + 0.9 * new_momentum)
    return (new_momentum, new_global)


def unpack(packed, scales):
    lower_code = packed % 16
    upper_code = packed // 16
    unpacked = jnp.stack([lower_code, upper_code], axis=-1).reshape(
        packed.shape[:-1] + (2 * packed.shape[-1],)
    )
    centered = (unpacked - 8).astype(jnp.float32)
    blocks = centered.reshape(packed.shape[:-1] + (scales.shape[-1], -1)) * scales[..., None]
    return blocks.reshape(unpacked.shape).astype(jnp.bfloat16)


def per_device_any(
    gate_pre, up_pre, out_grad, inner_params, global_params, outer_momentum, pair_codes, code_scales
):
    replicas = lax.axis_size("rep")
    tok_total = gate_pre.shape[0]
    unit_rows = gate_pre.shape[1]
    model_width = out_grad.shape[1]
    all_units = unit_rows * lax.axis_size("fsdp")
    gate_f32 = gate_pre.astype(jnp.float32)
    upper = up_pre.astype(jnp.float32)
    sigmoid_gate = jax.nn.sigmoid(gate_f32)
    hidden = (gate_f32 * sigmoid_gate * upper).astype(jnp.bfloat16)
    grads = lax.dot_general(
        hidden, out_grad, (((0,), (0,)), ((), ())), preferred_element_type=jnp.float32
    ) * (1.0 / tok_total)
    square_total = lax.psum(jnp.sum(grads * grads), "fsdp")
    root_mean = jnp.sqrt(square_total / (all_units * model_width) + 1e-06)
    clipped = grads * jnp.minimum(1.0, 0.02 / root_mean)
    pseudo = unpack(pair_codes[0], code_scales[0])
    delta_share = lax.psum_scatter(pseudo, "rep", scatter_dimension=1, tiled=True).astype(
        jnp.float32
    ) * (1.0 / replicas)
    new_momentum, new_global = outer_update(delta_share, outer_momentum, global_params)
    global_bf = lax.all_gather(new_global.astype(jnp.bfloat16), "rep", axis=1, tiled=True).astype(
        jnp.float32
    )
    master = inner_params[0].astype(jnp.float32)
    stepped = master - 0.8 * (clipped + 0.2 * master)
    merged_params = (0.5 * stepped + 0.5 * global_bf).astype(jnp.bfloat16)
    return (merged_params[None], new_global, new_momentum)


SLOTS = 4
MESH = pl.DeviceIdType.MESH


def fused_step(
    chunk, shards, tok_total, all_entries,
    gate, up, og, inner, glob, mom, codes, scales,
    merged_out, glob_out, mom_out,
    pseudo, ra, rb, sa, sb, r2a, r2b, gbf, glob_v, mom_v, code_v, scale_v,
    gate_v, up_v, og_v, hid_t, inner_v, merged_v, spread, squares, sums, factor,
    send_sem, recv_sem, sum_send, sum_recv, code_sem, load_sem, inner_sem, merged_sem, out_sem,
):
    rows = glob_v.shape[0]
    quarter = glob_v.shape[1]
    half = chunk // 2
    count = rows // chunk
    rep = lax.axis_index("rep")
    shard = lax.axis_index("fsdp")
    y, x = rep // 2, rep % 2
    x_peer, y_peer = y * 2 + (1 - x), (1 - y) * 2 + x

    def whole(c):
        return pl.ds(pl.multiple_of(c * chunk, chunk), chunk)

    def first(c):
        return pl.ds(pl.multiple_of(c * chunk, half), half)

    def second(c):
        return pl.ds(pl.multiple_of(c * chunk + half, half), half)

    def packed(c):
        return pl.ds(pl.multiple_of(c * half, half), half)

    def remote(src, dst, kind, c, peer):
        return pltpu.make_async_remote_copy(
            src_ref=src, dst_ref=dst, send_sem=send_sem.at[kind, c], recv_sem=recv_sem.at[kind, c],
            device_id=(peer, shard), device_id_type=MESH,
        )

    def scatter_x(c):
        return remote(pseudo.at[:, 1 - x, first(c)], ra.at[:, packed(c)], 0, c, x_peer)

    def scatter_y(c):
        return remote(pseudo.at[1 - y, :, second(c)], rb.at[:, packed(c)], 1, c, y_peer)

    def pass_y(c):
        return remote(sa.at[packed(c)], r2a.at[packed(c)], 2, c, y_peer)

    def pass_x(c):
        return remote(sb.at[packed(c)], r2b.at[packed(c)], 3, c, x_peer)

    def own_x(c, at_x):
        block = gbf.at[y, at_x, whole(c)]
        return remote(block, block, 4, c, x_peer)

    def own_y(c, at_y):
        block = gbf.at[at_y, x, whole(c)]
        return remote(block, block, 5, c, y_peer)

    def onward_x(c, at_x):
        block = gbf.at[1 - y, at_x, first(c)]
        return remote(block, block, 6, c, x_peer)

    def onward_y(c, at_y):
        block = gbf.at[at_y, 1 - x, second(c)]
        return remote(block, block, 7, c, y_peer)

    def sum_copy(step):
        return pltpu.make_async_remote_copy(
            src_ref=sums.at[0], dst_ref=sums.at[step],
            send_sem=sum_send.at[step - 1], recv_sem=sum_recv.at[step - 1],
            device_id=(rep, (shard + step) % shards), device_id_type=MESH,
        )

    def code_copy(c):
        return pltpu.make_async_copy(
            codes.at[whole(c)], code_v.at[c % SLOTS], code_sem.at[c % SLOTS]
        )

    def inner_copy(c):
        return pltpu.make_async_copy(inner.at[whole(c)], inner_v.at[c % 2], inner_sem.at[c % 2])

    def merged_copy(c):
        return pltpu.make_async_copy(
            merged_v.at[c % 2], merged_out.at[whole(c)], merged_sem.at[c % 2]
        )

    def glob_copy(c):
        return pltpu.make_async_copy(glob_v.at[whole(c)], glob_out.at[whole(c)], out_sem.at[0, c])

    def mom_copy(c):
        return pltpu.make_async_copy(mom_v.at[whole(c)], mom_out.at[whole(c)], out_sem.at[1, c])

    barrier = pltpu.get_barrier_semaphore()
    for peer in (x_peer, y_peer):
        pl.semaphore_signal(barrier, inc=1, device_id=(peer, shard), device_id_type=MESH)
    for step in range(1, shards):
        pl.semaphore_signal(
            barrier, inc=1, device_id=(rep, (shard + step) % shards), device_id_type=MESH
        )

    scale_load = pltpu.make_async_copy(scales, scale_v, load_sem.at[0])
    gate_load = pltpu.make_async_copy(gate, gate_v, load_sem.at[1])
    up_load = pltpu.make_async_copy(up, up_v, load_sem.at[2])
    og_load = pltpu.make_async_copy(og, og_v, load_sem.at[3])
    glob_load = pltpu.make_async_copy(glob, glob_v, load_sem.at[4])
    mom_load = pltpu.make_async_copy(mom, mom_v, load_sem.at[5])
    scale_load.start()
    for c in range(min(SLOTS, count)):
        code_copy(c).start()
    for load in (gate_load, up_load, og_load, glob_load, mom_load):
        load.start()
    for c in range(min(2, count)):
        inner_copy(c).start()

    k = lax.broadcasted_iota(jnp.int32, (256, 256), 0)
    n = lax.broadcasted_iota(jnp.int32, (256, 256), 1)
    j, odd = n >> 1, n & 1
    from_word = jnp.where((k == j) & (odd == 0), 1.0, 0.0)
    from_upper = jnp.where(k == j + 128, jnp.where(odd == 0, -16.0, 1.0), 0.0)
    spread[...] = (from_word + from_upper).astype(jnp.bfloat16)
    squares[...] = jnp.zeros_like(squares)

    scale_load.wait()
    pl.semaphore_wait(barrier, shards + 1)

    def unpack_chunk(c, carry):
        code_copy(c).wait()
        slot = c % SLOTS
        for b in range(code_v.shape[2] // 128):
            word = code_v[slot, :, 128 * b : 128 * b + 128]
            pair = jnp.concatenate(
                [
                    (word - 136).astype(jnp.float32).astype(jnp.bfloat16),
                    ((word >> 4) - 8).astype(jnp.float32).astype(jnp.bfloat16),
                ],
                axis=1,
            )
            centered = jnp.dot(pair, spread[...], preferred_element_type=jnp.float32)
            for part in range(2):
                col = 256 * b + 128 * part
                q, at = col // quarter, col % quarter
                value = centered[:, 128 * part : 128 * part + 128]
                value = value * scale_v[whole(c), 2 * b + part : 2 * b + part + 1]
                pseudo[q // 2, q % 2, whole(c), at : at + 128] = value.astype(jnp.bfloat16)
        scatter_x(c).start()
        scatter_y(c).start()

        @pl.when(c + SLOTS < count)
        def _():
            code_copy(c + SLOTS).start()

        return carry

    lax.fori_loop(0, count, unpack_chunk, 0)

    gate_load.wait()
    up_load.wait()
    og_load.wait()

    def square_chunk(c, carry):
        cols = whole(c)
        g = gate_v[:, cols].astype(jnp.float32)
        h = g * jax.nn.sigmoid(g) * up_v[:, cols].astype(jnp.float32)
        hid_t[cols, :] = h.T.astype(jnp.bfloat16)
        for q in range(4):
            grad = jnp.dot(
                hid_t[cols, :], og_v[:, quarter * q : quarter * (q + 1)],
                preferred_element_type=jnp.float32,
            ) * (1.0 / tok_total)
            squares[...] += jnp.sum((grad * grad).reshape(chunk // 8, 8, quarter), axis=0)
        return carry

    lax.fori_loop(0, count, square_chunk, 0)
    sums[0] = jnp.full((8, 128), jnp.sum(squares[...]), jnp.float32)
    for step in range(1, shards):
        sum_copy(step).start()

    def pass_chunk(c, carry):
        scatter_x(c).wait_recv()
        mine = pseudo[1 - y, x, first(c)].astype(jnp.float32)
        sa[packed(c)] = (mine + ra[1 - y, packed(c)].astype(jnp.float32)).astype(jnp.bfloat16)
        pass_y(c).start()
        scatter_y(c).wait_recv()
        mine = pseudo[y, 1 - x, second(c)].astype(jnp.float32)
        sb[packed(c)] = (mine + rb[1 - x, packed(c)].astype(jnp.float32)).astype(jnp.bfloat16)
        pass_x(c).start()
        return carry

    lax.fori_loop(0, count, pass_chunk, 0)
    glob_load.wait()
    mom_load.wait()

    def outer_rows(at, total):
        new_momentum, new_global = outer_update(total * 0.25, mom_v[at], glob_v[at])
        mom_v[at] = new_momentum
        glob_v[at] = new_global
        gbf[y, x, at] = new_global.astype(jnp.bfloat16)

    def outer_chunk(c, carry):
        f32 = jnp.float32
        pass_y(c).wait_recv()
        at, near = first(c), packed(c)
        outer_rows(at, pseudo[y, x, at].astype(f32) + ra[y, near].astype(f32) + r2a[near].astype(f32))
        pass_x(c).wait_recv()
        at = second(c)
        outer_rows(at, pseudo[y, x, at].astype(f32) + rb[x, near].astype(f32) + r2b[near].astype(f32))
        own_x(c, x).start()
        own_y(c, y).start()
        glob_copy(c).start()
        mom_copy(c).start()
        return carry

    lax.fori_loop(0, count, outer_chunk, 0)

    for step in range(1, shards):
        sum_copy(step).wait_recv()
    total = sums[0]
    for step in range(1, shards):
        total = total + sums[step]
    root_mean = jnp.sqrt(total / all_entries + 1e-06)
    scale = jnp.minimum(1.0, 0.02 / root_mean) * (0.4 / tok_total)
    factor[...] = jnp.concatenate([scale] * (quarter // 128), axis=1)

    def onward_chunk(c, carry):
        own_y(c, 1 - y).wait_recv()
        onward_x(c, x).start()
        own_x(c, 1 - x).wait_recv()
        onward_y(c, y).start()
        return carry

    lax.fori_loop(0, count, onward_chunk, 0)

    def merge_chunk(c, carry):
        slot = c % 2
        inner_copy(c).wait()

        @pl.when(c >= 2)
        def _():
            merged_copy(c - 2).wait()

        onward_x(c, 1 - x).wait_recv()
        onward_y(c, 1 - y).wait_recv()
        for q in range(4):
            cols = slice(quarter * q, quarter * (q + 1))
            grad = jnp.dot(hid_t[whole(c), :], og_v[:, cols], preferred_element_type=jnp.float32)
            kept = 0.42 * inner_v[slot, :, cols].astype(jnp.float32)
            kept = kept + 0.5 * gbf[q // 2, q % 2, whole(c)].astype(jnp.float32)
            merged_v[slot, :, cols] = (kept - grad * factor[0:1, :]).astype(jnp.bfloat16)
        merged_copy(c).start()

        @pl.when(c + 2 < count)
        def _():
            inner_copy(c + 2).start()

        return carry

    lax.fori_loop(0, count, merge_chunk, 0)
    for c in range(max(count - 2, 0), count):
        merged_copy(c).wait()

    def drain(c, carry):
        scatter_x(c).wait_send()
        scatter_y(c).wait_send()
        pass_y(c).wait_send()
        pass_x(c).wait_send()
        own_x(c, x).wait_send()
        own_y(c, y).wait_send()
        onward_x(c, x).wait_send()
        onward_y(c, y).wait_send()
        glob_copy(c).wait()
        mom_copy(c).wait()
        return carry

    lax.fori_loop(0, count, drain, 0)
    for step in range(1, shards):
        sum_copy(step).wait_send()


def per_device_square(
    gate_pre, up_pre, out_grad, inner_params, global_params, outer_momentum, pair_codes, code_scales
):
    shards = lax.axis_size("fsdp")
    tokens, rows = gate_pre.shape
    width = out_grad.shape[1]
    quarter = width // 4
    chunk = 128
    count = rows // chunk
    bf16, f32 = jnp.bfloat16, jnp.float32
    dma = pltpu.SemaphoreType.DMA
    any_spec = pl.BlockSpec(memory_space=pl.ANY)
    merged, new_global, new_momentum = pl.pallas_call(
        functools.partial(fused_step, chunk, shards, tokens, rows * shards * width),
        out_shape=(
            jax.ShapeDtypeStruct((rows, width), bf16),
            jax.ShapeDtypeStruct((rows, quarter), f32),
            jax.ShapeDtypeStruct((rows, quarter), f32),
        ),
        in_specs=[any_spec] * 8,
        out_specs=(any_spec,) * 3,
        scratch_shapes=[
            pltpu.VMEM((2, 2, rows, quarter), bf16),
            pltpu.VMEM((2, rows // 2, quarter), bf16),
            pltpu.VMEM((2, rows // 2, quarter), bf16),
            pltpu.VMEM((rows // 2, quarter), bf16),
            pltpu.VMEM((rows // 2, quarter), bf16),
            pltpu.VMEM((rows // 2, quarter), bf16),
            pltpu.VMEM((rows // 2, quarter), bf16),
            pltpu.VMEM((2, 2, rows, quarter), bf16),
            pltpu.VMEM((rows, quarter), f32),
            pltpu.VMEM((rows, quarter), f32),
            pltpu.VMEM((SLOTS, chunk, width // 2), jnp.int32),
            pltpu.VMEM(code_scales.shape[1:], f32),
            pltpu.VMEM((tokens, rows), bf16),
            pltpu.VMEM((tokens, rows), bf16),
            pltpu.VMEM((tokens, width), bf16),
            pltpu.VMEM((rows, tokens), bf16),
            pltpu.VMEM((2, chunk, width), bf16),
            pltpu.VMEM((2, chunk, width), bf16),
            pltpu.VMEM((256, 256), bf16),
            pltpu.VMEM((8, quarter), f32),
            pltpu.VMEM((shards, 8, 128), f32),
            pltpu.VMEM((8, quarter), f32),
            dma((8, count)),
            dma((8, count)),
            dma((shards - 1,)),
            dma((shards - 1,)),
            dma((SLOTS,)),
            dma((6,)),
            dma((2,)),
            dma((2,)),
            dma((2, count)),
        ],
        compiler_params=pltpu.CompilerParams(
            collective_id=0, has_side_effects=True, vmem_limit_bytes=60 * 1024 * 1024
        ),
        cost_estimate=pl.CostEstimate(
            flops=4 * tokens * rows * width, bytes_accessed=22 * rows * width, transcendentals=0
        ),
    )(
        gate_pre, up_pre, out_grad, inner_params[0], global_params, outer_momentum,
        pair_codes[0], code_scales[0],
    )
    return (merged[None], new_global, new_momentum)


def per_device(*arrays):
    rows, width = arrays[0].shape[1], arrays[2].shape[1]
    square = lax.axis_size("rep") == 4 and lax.axis_size("fsdp") > 1
    if square and rows % 128 == 0 and width % 1024 == 0 and width // arrays[7].shape[2] == 128:
        return per_device_square(*arrays)
    return per_device_any(*arrays)


def solution(mesh):
    in_specs = (
        P("rep", "fsdp"),
        P("rep", "fsdp"),
        P("rep", None),
        P("rep", "fsdp", None),
        P("fsdp", "rep"),
        P("fsdp", "rep"),
        P("rep", "fsdp", None),
        P("rep", "fsdp", None),
    )
    out_specs = (P("rep", "fsdp", None), P("fsdp", "rep"), P("fsdp", "rep"))
    return jax.shard_map(
        per_device, mesh=mesh, in_specs=in_specs, out_specs=out_specs, check_vma=False
    )
```

```python
import functools
import jax
import jax.numpy as jnp
from jax import lax
from jax.experimental import pallas as pl
from jax.experimental.pallas import tpu as pltpu
from jax.sharding import PartitionSpec as P


def outer_update(mean_delta, momentum, params):
    new_momentum = 0.9 * momentum + mean_delta
    new_global = params - 0.7 * (mean_delta + 0.9 * new_momentum)
    return (new_momentum, new_global)


def unpack(packed, scales):
    lower_code = packed % 16
    upper_code = packed // 16
    unpacked = jnp.stack([lower_code, upper_code], axis=-1).reshape(
        packed.shape[:-1] + (2 * packed.shape[-1],)
    )
    centered = (unpacked - 8).astype(jnp.float32)
    blocks = centered.reshape(packed.shape[:-1] + (scales.shape[-1], -1)) * scales[..., None]
    return blocks.reshape(unpacked.shape).astype(jnp.bfloat16)


def per_device_any(
    gate_pre, up_pre, out_grad, inner_params, global_params, outer_momentum, pair_codes, code_scales
):
    replicas = lax.axis_size("rep")
    tok_total = gate_pre.shape[0]
    unit_rows = gate_pre.shape[1]
    model_width = out_grad.shape[1]
    all_units = unit_rows * lax.axis_size("fsdp")
    gate_f32 = gate_pre.astype(jnp.float32)
    upper = up_pre.astype(jnp.float32)
    sigmoid_gate = jax.nn.sigmoid(gate_f32)
    hidden = (gate_f32 * sigmoid_gate * upper).astype(jnp.bfloat16)
    grads = lax.dot_general(
        hidden, out_grad, (((0,), (0,)), ((), ())), preferred_element_type=jnp.float32
    ) * (1.0 / tok_total)
    square_total = lax.psum(jnp.sum(grads * grads), "fsdp")
    root_mean = jnp.sqrt(square_total / (all_units * model_width) + 1e-06)
    clipped = grads * jnp.minimum(1.0, 0.02 / root_mean)
    pseudo = unpack(pair_codes[0], code_scales[0])
    delta_share = lax.psum_scatter(pseudo, "rep", scatter_dimension=1, tiled=True).astype(
        jnp.float32
    ) * (1.0 / replicas)
    new_momentum, new_global = outer_update(delta_share, outer_momentum, global_params)
    global_bf = lax.all_gather(new_global.astype(jnp.bfloat16), "rep", axis=1, tiled=True).astype(
        jnp.float32
    )
    master = inner_params[0].astype(jnp.float32)
    stepped = master - 0.8 * (clipped + 0.2 * master)
    merged_params = (0.5 * stepped + 0.5 * global_bf).astype(jnp.bfloat16)
    return (merged_params[None], new_global, new_momentum)


SLOTS = 4
MESH = pl.DeviceIdType.MESH


def fused_step(
    chunk, shards, tok_total, all_entries,
    gate, up, og, inner, glob, mom, codes, scales,
    pseudo, glob_v, mom_v,
    ra, rb, sa, sb, r2a, r2b, gbf, code_v, scale_v,
    gate_v, up_v, og_v, hid_t, inner_v, spread, squares, sums, factor,
    send_sem, recv_sem, sum_send, sum_recv, code_sem, load_sem, inner_sem,
):
    rows = glob_v.shape[0]
    quarter = glob_v.shape[1]
    half = chunk // 2
    count = rows // chunk
    rep = lax.axis_index("rep")
    shard = lax.axis_index("fsdp")
    y, x = rep // 2, rep % 2
    x_peer, y_peer = y * 2 + (1 - x), (1 - y) * 2 + x

    def whole(c):
        return pl.ds(pl.multiple_of(c * chunk, chunk), chunk)

    def first(c):
        return pl.ds(pl.multiple_of(c * chunk, half), half)

    def second(c):
        return pl.ds(pl.multiple_of(c * chunk + half, half), half)

    def packed(c):
        return pl.ds(pl.multiple_of(c * half, half), half)

    def remote(src, dst, kind, c, peer):
        return pltpu.make_async_remote_copy(
            src_ref=src, dst_ref=dst, send_sem=send_sem.at[kind, c], recv_sem=recv_sem.at[kind, c],
            device_id=(peer, shard), device_id_type=MESH,
        )

    def scatter_x(c):
        return remote(pseudo.at[:, 1 - x, first(c)], ra.at[:, packed(c)], 0, c, x_peer)

    def scatter_y(c):
        return remote(pseudo.at[1 - y, :, second(c)], rb.at[:, packed(c)], 1, c, y_peer)

    def pass_y(c):
        return remote(sa.at[packed(c)], r2a.at[packed(c)], 2, c, y_peer)

    def pass_x(c):
        return remote(sb.at[packed(c)], r2b.at[packed(c)], 3, c, x_peer)

    def own_x(c, at_x):
        block = gbf.at[y, at_x, whole(c)]
        return remote(block, block, 4, c, x_peer)

    def own_y(c, at_y):
        block = gbf.at[at_y, x, whole(c)]
        return remote(block, block, 5, c, y_peer)

    def onward_x(c, at_x):
        block = gbf.at[1 - y, at_x, first(c)]
        return remote(block, block, 6, c, x_peer)

    def onward_y(c, at_y):
        block = gbf.at[at_y, 1 - x, second(c)]
        return remote(block, block, 7, c, y_peer)

    def sum_copy(step):
        return pltpu.make_async_remote_copy(
            src_ref=sums.at[0], dst_ref=sums.at[step],
            send_sem=sum_send.at[step - 1], recv_sem=sum_recv.at[step - 1],
            device_id=(rep, (shard + step) % shards), device_id_type=MESH,
        )

    def code_copy(c):
        return pltpu.make_async_copy(
            codes.at[whole(c)], code_v.at[c % SLOTS], code_sem.at[c % SLOTS]
        )

    def inner_copy(c):
        return pltpu.make_async_copy(inner.at[whole(c)], inner_v.at[c % 2], inner_sem.at[c % 2])

    barrier = pltpu.get_barrier_semaphore()
    for peer in (x_peer, y_peer):
        pl.semaphore_signal(barrier, inc=1, device_id=(peer, shard), device_id_type=MESH)
    for step in range(1, shards):
        pl.semaphore_signal(
            barrier, inc=1, device_id=(rep, (shard + step) % shards), device_id_type=MESH
        )

    scale_load = pltpu.make_async_copy(scales, scale_v, load_sem.at[0])
    gate_load = pltpu.make_async_copy(gate, gate_v, load_sem.at[1])
    up_load = pltpu.make_async_copy(up, up_v, load_sem.at[2])
    og_load = pltpu.make_async_copy(og, og_v, load_sem.at[3])
    glob_load = pltpu.make_async_copy(glob, glob_v, load_sem.at[4])
    mom_load = pltpu.make_async_copy(mom, mom_v, load_sem.at[5])
    scale_load.start()
    for c in range(min(SLOTS, count)):
        code_copy(c).start()
    for load in (gate_load, up_load, og_load, glob_load, mom_load):
        load.start()
    for c in range(min(2, count)):
        inner_copy(c).start()

    k = lax.broadcasted_iota(jnp.int32, (256, 256), 0)
    n = lax.broadcasted_iota(jnp.int32, (256, 256), 1)
    j, odd = n >> 1, n & 1
    from_word = jnp.where((k == j) & (odd == 0), 1.0, 0.0)
    from_upper = jnp.where(k == j + 128, jnp.where(odd == 0, -16.0, 1.0), 0.0)
    spread[...] = (from_word + from_upper).astype(jnp.bfloat16)
    squares[...] = jnp.zeros_like(squares)

    scale_load.wait()
    pl.semaphore_wait(barrier, shards + 1)

    def unpack_chunk(c, carry):
        code_copy(c).wait()
        block_scale = scale_v[:, whole(c)].T
        slot = c % SLOTS
        for b in range(code_v.shape[2] // 128):
            word = code_v[slot, :, 128 * b : 128 * b + 128]
            pair = jnp.concatenate(
                [
                    (word - 136).astype(jnp.float32).astype(jnp.bfloat16),
                    ((word >> 4) - 8).astype(jnp.float32).astype(jnp.bfloat16),
                ],
                axis=1,
            )
            centered = jnp.dot(pair, spread[...], preferred_element_type=jnp.float32)
            for part in range(2):
                col = 256 * b + 128 * part
                q, at = col // quarter, col % quarter
                value = centered[:, 128 * part : 128 * part + 128]
                value = value * block_scale[:, 2 * b + part : 2 * b + part + 1]
                pseudo[q // 2, q % 2, whole(c), at : at + 128] = value.astype(jnp.bfloat16)
        scatter_x(c).start()
        scatter_y(c).start()

        @pl.when(c + SLOTS < count)
        def _():
            code_copy(c + SLOTS).start()

        return carry

    lax.fori_loop(0, count, unpack_chunk, 0)

    gate_load.wait()
    up_load.wait()
    og_load.wait()

    def square_chunk(c, carry):
        cols = whole(c)
        g = gate_v[:, cols].astype(jnp.float32)
        h = g * jax.nn.sigmoid(g) * up_v[:, cols].astype(jnp.float32)
        hid_t[cols, :] = h.T.astype(jnp.bfloat16)
        for q in range(4):
            grad = jnp.dot(
                hid_t[cols, :], og_v[:, quarter * q : quarter * (q + 1)],
                preferred_element_type=jnp.float32,
            ) * (1.0 / tok_total)
            squares[...] += jnp.sum((grad * grad).reshape(chunk // 8, 8, quarter), axis=0)
        return carry

    lax.fori_loop(0, count, square_chunk, 0)
    sums[0] = jnp.full((8, 128), jnp.sum(squares[...]), jnp.float32)
    for step in range(1, shards):
        sum_copy(step).start()

    def pass_chunk(c, carry):
        scatter_x(c).wait_recv()
        mine = pseudo[1 - y, x, first(c)].astype(jnp.float32)
        sa[packed(c)] = (mine + ra[1 - y, packed(c)].astype(jnp.float32)).astype(jnp.bfloat16)
        pass_y(c).start()
        scatter_y(c).wait_recv()
        mine = pseudo[y, 1 - x, second(c)].astype(jnp.float32)
        sb[packed(c)] = (mine + rb[1 - x, packed(c)].astype(jnp.float32)).astype(jnp.bfloat16)
        pass_x(c).start()
        return carry

    lax.fori_loop(0, count, pass_chunk, 0)
    glob_load.wait()
    mom_load.wait()

    def outer_rows(at, total):
        new_momentum, new_global = outer_update(total * 0.25, mom_v[at], glob_v[at])
        mom_v[at] = new_momentum
        glob_v[at] = new_global
        gbf[y, x, at] = new_global.astype(jnp.bfloat16)

    def outer_chunk(c, carry):
        f32 = jnp.float32
        pass_y(c).wait_recv()
        at, near = first(c), packed(c)
        outer_rows(at, pseudo[y, x, at].astype(f32) + ra[y, near].astype(f32) + r2a[near].astype(f32))
        pass_x(c).wait_recv()
        at = second(c)
        outer_rows(at, pseudo[y, x, at].astype(f32) + rb[x, near].astype(f32) + r2b[near].astype(f32))
        own_x(c, x).start()
        own_y(c, y).start()
        return carry

    lax.fori_loop(0, count, outer_chunk, 0)

    for step in range(1, shards):
        sum_copy(step).wait_recv()
    total = sums[0]
    for step in range(1, shards):
        total = total + sums[step]
    root_mean = jnp.sqrt(total / all_entries + 1e-06)
    scale = jnp.minimum(1.0, 0.02 / root_mean) * (0.4 / tok_total)
    factor[...] = jnp.concatenate([scale] * (quarter // 128), axis=1)

    def onward_chunk(c, carry):
        own_y(c, 1 - y).wait_recv()
        onward_x(c, x).start()
        own_x(c, 1 - x).wait_recv()
        onward_y(c, y).start()
        return carry

    lax.fori_loop(0, count, onward_chunk, 0)

    def merge_chunk(c, carry):
        slot = c % 2
        inner_copy(c).wait()

        scatter_x(c).wait_send()
        scatter_y(c).wait_send()
        onward_x(c, 1 - x).wait_recv()
        onward_y(c, 1 - y).wait_recv()
        for q in range(4):
            cols = slice(quarter * q, quarter * (q + 1))
            grad = jnp.dot(hid_t[whole(c), :], og_v[:, cols], preferred_element_type=jnp.float32)
            kept = 0.42 * inner_v[slot, :, cols].astype(jnp.float32)
            kept = kept + 0.5 * gbf[q // 2, q % 2, whole(c)].astype(jnp.float32)
            pseudo[q // 2, q % 2, whole(c)] = (kept - grad * factor[0:1, :]).astype(jnp.bfloat16)

        @pl.when(c + 2 < count)
        def _():
            inner_copy(c + 2).start()

        return carry

    lax.fori_loop(0, count, merge_chunk, 0)

    def drain(c, carry):
        pass_y(c).wait_send()
        pass_x(c).wait_send()
        own_x(c, x).wait_send()
        own_y(c, y).wait_send()
        onward_x(c, x).wait_send()
        onward_y(c, y).wait_send()
        return carry

    lax.fori_loop(0, count, drain, 0)
    for step in range(1, shards):
        sum_copy(step).wait_send()


def write_results(merged_v, glob_v, mom_v, merged_out, glob_out, mom_out, sem):
    rows, quarter = glob_v.shape
    copies = []
    for q in range(4):
        place = merged_out.at[:, pl.ds(quarter * q, quarter)]
        copies.append(pltpu.make_async_copy(merged_v.at[q // 2, q % 2], place, sem.at[q]))
    for index, (held, out) in enumerate(((glob_v, glob_out), (mom_v, mom_out))):
        for part in range(2):
            at = pl.ds(part * (rows // 2), rows // 2)
            copies.append(
                pltpu.make_async_copy(held.at[at], out.at[at], sem.at[4 + 2 * index + part])
            )
    for copy in copies:
        copy.start()
    for copy in copies:
        copy.wait()


def per_device_square(
    gate_pre, up_pre, out_grad, inner_params, global_params, outer_momentum, pair_codes, code_scales
):
    shards = lax.axis_size("fsdp")
    tokens, rows = gate_pre.shape
    width = out_grad.shape[1]
    quarter = width // 4
    chunk = 128
    count = rows // chunk
    bf16, f32 = jnp.bfloat16, jnp.float32
    dma = pltpu.SemaphoreType.DMA
    any_spec = pl.BlockSpec(memory_space=pl.ANY)
    vmem_spec = pl.BlockSpec(memory_space=pltpu.VMEM)
    merged, new_global, new_momentum = pl.pallas_call(
        functools.partial(fused_step, chunk, shards, tokens, rows * shards * width),
        out_shape=(
            pltpu.VMEM((2, 2, rows, quarter), bf16),
            pltpu.VMEM((rows, quarter), f32),
            pltpu.VMEM((rows, quarter), f32),
        ),
        in_specs=[any_spec] * 8,
        out_specs=(vmem_spec,) * 3,
        scratch_shapes=[
            pltpu.VMEM((2, rows // 2, quarter), bf16),
            pltpu.VMEM((2, rows // 2, quarter), bf16),
            pltpu.VMEM((rows // 2, quarter), bf16),
            pltpu.VMEM((rows // 2, quarter), bf16),
            pltpu.VMEM((rows // 2, quarter), bf16),
            pltpu.VMEM((rows // 2, quarter), bf16),
            pltpu.VMEM((2, 2, rows, quarter), bf16),
            pltpu.VMEM((SLOTS, chunk, width // 2), jnp.int32),
            pltpu.VMEM((code_scales.shape[2], rows), f32),
            pltpu.VMEM((tokens, rows), bf16),
            pltpu.VMEM((tokens, rows), bf16),
            pltpu.VMEM((tokens, width), bf16),
            pltpu.VMEM((rows, tokens), bf16),
            pltpu.VMEM((2, chunk, width), bf16),
            pltpu.VMEM((256, 256), bf16),
            pltpu.VMEM((8, quarter), f32),
            pltpu.VMEM((shards, 8, 128), f32),
            pltpu.VMEM((8, quarter), f32),
            dma((8, count)),
            dma((8, count)),
            dma((shards - 1,)),
            dma((shards - 1,)),
            dma((SLOTS,)),
            dma((6,)),
            dma((2,)),
        ],
        compiler_params=pltpu.CompilerParams(
            collective_id=0, has_side_effects=True, vmem_limit_bytes=40 * 1024 * 1024
        ),
        cost_estimate=pl.CostEstimate(
            flops=4 * tokens * rows * width, bytes_accessed=22 * rows * width, transcendentals=0
        ),
    )(
        gate_pre, up_pre, out_grad, inner_params[0], global_params, outer_momentum,
        pair_codes[0], code_scales[0].T,
    )
    merged, new_global, new_momentum = pl.pallas_call(
        write_results,
        out_shape=(
            jax.ShapeDtypeStruct((rows, width), bf16),
            jax.ShapeDtypeStruct((rows, quarter), f32),
            jax.ShapeDtypeStruct((rows, quarter), f32),
        ),
        in_specs=[vmem_spec] * 3,
        out_specs=(any_spec,) * 3,
        scratch_shapes=[dma((8,))],
        compiler_params=pltpu.CompilerParams(vmem_limit_bytes=4 * 1024 * 1024),
        cost_estimate=pl.CostEstimate(
            flops=0, bytes_accessed=4 * rows * width, transcendentals=0
        ),
    )(merged, new_global, new_momentum)
    return (merged[None], new_global, new_momentum)


def per_device(*arrays):
    rows, width = arrays[0].shape[1], arrays[2].shape[1]
    square = lax.axis_size("rep") == 4 and lax.axis_size("fsdp") > 1
    if square and rows % 128 == 0 and width % 1024 == 0 and width // arrays[7].shape[2] == 128:
        return per_device_square(*arrays)
    return per_device_any(*arrays)


def solution(mesh):
    in_specs = (
        P("rep", "fsdp"),
        P("rep", "fsdp"),
        P("rep", None),
        P("rep", "fsdp", None),
        P("fsdp", "rep"),
        P("fsdp", "rep"),
        P("rep", "fsdp", None),
        P("rep", "fsdp", None),
    )
    out_specs = (P("rep", "fsdp", None), P("fsdp", "rep"), P("fsdp", "rep"))
    return jax.shard_map(
        per_device, mesh=mesh, in_specs=in_specs, out_specs=out_specs, check_vma=False
    )
```

```python
import functools
import jax
import jax.numpy as jnp
from jax import lax
from jax.experimental import pallas as pl
from jax.experimental.pallas import tpu as pltpu
from jax.sharding import PartitionSpec as P


def outer_update(mean_delta, momentum, params):
    new_momentum = 0.9 * momentum + mean_delta
    new_global = params - 0.7 * (mean_delta + 0.9 * new_momentum)
    return (new_momentum, new_global)


def unpack(packed, scales):
    lower_code = packed % 16
    upper_code = packed // 16
    unpacked = jnp.stack([lower_code, upper_code], axis=-1).reshape(
        packed.shape[:-1] + (2 * packed.shape[-1],)
    )
    centered = (unpacked - 8).astype(jnp.float32)
    blocks = centered.reshape(packed.shape[:-1] + (scales.shape[-1], -1)) * scales[..., None]
    return blocks.reshape(unpacked.shape).astype(jnp.bfloat16)


def per_device_any(
    gate_pre, up_pre, out_grad, inner_params, global_params, outer_momentum, pair_codes, code_scales
):
    replicas = lax.axis_size("rep")
    tok_total = gate_pre.shape[0]
    unit_rows = gate_pre.shape[1]
    model_width = out_grad.shape[1]
    all_units = unit_rows * lax.axis_size("fsdp")
    gate_f32 = gate_pre.astype(jnp.float32)
    upper = up_pre.astype(jnp.float32)
    sigmoid_gate = jax.nn.sigmoid(gate_f32)
    hidden = (gate_f32 * sigmoid_gate * upper).astype(jnp.bfloat16)
    grads = lax.dot_general(
        hidden, out_grad, (((0,), (0,)), ((), ())), preferred_element_type=jnp.float32
    ) * (1.0 / tok_total)
    square_total = lax.psum(jnp.sum(grads * grads), "fsdp")
    root_mean = jnp.sqrt(square_total / (all_units * model_width) + 1e-06)
    clipped = grads * jnp.minimum(1.0, 0.02 / root_mean)
    pseudo = unpack(pair_codes[0], code_scales[0])
    delta_share = lax.psum_scatter(pseudo, "rep", scatter_dimension=1, tiled=True).astype(
        jnp.float32
    ) * (1.0 / replicas)
    new_momentum, new_global = outer_update(delta_share, outer_momentum, global_params)
    global_bf = lax.all_gather(new_global.astype(jnp.bfloat16), "rep", axis=1, tiled=True).astype(
        jnp.float32
    )
    master = inner_params[0].astype(jnp.float32)
    stepped = master - 0.8 * (clipped + 0.2 * master)
    merged_params = (0.5 * stepped + 0.5 * global_bf).astype(jnp.bfloat16)
    return (merged_params[None], new_global, new_momentum)


SLOTS = 4
LAG = 2
MESH = pl.DeviceIdType.MESH


def fused_step(
    chunk, shards, tok_total, all_entries,
    gate, up, og, inner, glob, mom, codes, scales,
    pseudo, glob_v, mom_v,
    ra, rb, sa, sb, r2a, r2b, gbf, code_v, scale_v,
    gate_v, up_v, og_v, hid_t, inner_v, spread, squares, sums, factor,
    send_sem, recv_sem, sum_send, sum_recv, code_sem, load_sem, inner_sem,
):
    rows = glob_v.shape[0]
    quarter = glob_v.shape[1]
    half = chunk // 2
    count = rows // chunk
    rep = lax.axis_index("rep")
    shard = lax.axis_index("fsdp")
    y, x = rep // 2, rep % 2
    x_peer, y_peer = y * 2 + (1 - x), (1 - y) * 2 + x

    def whole(c):
        return pl.ds(pl.multiple_of(c * chunk, chunk), chunk)

    def first(c):
        return pl.ds(pl.multiple_of(c * chunk, half), half)

    def second(c):
        return pl.ds(pl.multiple_of(c * chunk + half, half), half)

    def packed(c):
        return pl.ds(pl.multiple_of(c * half, half), half)

    def remote(src, dst, kind, c, peer):
        return pltpu.make_async_remote_copy(
            src_ref=src, dst_ref=dst, send_sem=send_sem.at[kind, c], recv_sem=recv_sem.at[kind, c],
            device_id=(peer, shard), device_id_type=MESH,
        )

    def scatter_x(c):
        return remote(pseudo.at[:, 1 - x, first(c)], ra.at[:, packed(c)], 0, c, x_peer)

    def scatter_y(c):
        return remote(pseudo.at[1 - y, :, second(c)], rb.at[:, packed(c)], 1, c, y_peer)

    def pass_y(c):
        return remote(sa.at[packed(c)], r2a.at[packed(c)], 2, c, y_peer)

    def pass_x(c):
        return remote(sb.at[packed(c)], r2b.at[packed(c)], 3, c, x_peer)

    def own_x(c, at_x):
        block = gbf.at[y, at_x, whole(c)]
        return remote(block, block, 4, c, x_peer)

    def own_y(c, at_y):
        block = gbf.at[at_y, x, whole(c)]
        return remote(block, block, 5, c, y_peer)

    def onward_x(c, at_x):
        block = gbf.at[1 - y, at_x, first(c)]
        return remote(block, block, 6, c, x_peer)

    def onward_y(c, at_y):
        block = gbf.at[at_y, 1 - x, second(c)]
        return remote(block, block, 7, c, y_peer)

    def sum_copy(step):
        return pltpu.make_async_remote_copy(
            src_ref=sums.at[0], dst_ref=sums.at[step],
            send_sem=sum_send.at[step - 1], recv_sem=sum_recv.at[step - 1],
            device_id=(rep, (shard + step) % shards), device_id_type=MESH,
        )

    def code_copy(c):
        return pltpu.make_async_copy(
            codes.at[whole(c)], code_v.at[c % SLOTS], code_sem.at[c % SLOTS]
        )

    def inner_copy(c):
        return pltpu.make_async_copy(inner.at[whole(c)], inner_v.at[c % 2], inner_sem.at[c % 2])

    scale_load = pltpu.make_async_copy(scales, scale_v, load_sem.at[0])
    gate_load = pltpu.make_async_copy(gate, gate_v, load_sem.at[1])
    up_load = pltpu.make_async_copy(up, up_v, load_sem.at[2])
    og_load = pltpu.make_async_copy(og, og_v, load_sem.at[3])
    glob_load = pltpu.make_async_copy(glob, glob_v, load_sem.at[4])
    mom_load = pltpu.make_async_copy(mom, mom_v, load_sem.at[5])
    code_copy(0).start()
    scale_load.start()
    for c in range(1, min(SLOTS, count)):
        code_copy(c).start()

    barrier = pltpu.get_barrier_semaphore()
    for peer in (x_peer, y_peer):
        pl.semaphore_signal(barrier, inc=1, device_id=(peer, shard), device_id_type=MESH)
    for step in range(1, shards):
        pl.semaphore_signal(
            barrier, inc=1, device_id=(rep, (shard + step) % shards), device_id_type=MESH
        )

    k = lax.broadcasted_iota(jnp.int32, (256, 256), 0)
    n = lax.broadcasted_iota(jnp.int32, (256, 256), 1)
    j, odd = n >> 1, n & 1
    from_word = jnp.where((k == j) & (odd == 0), 1.0, 0.0)
    from_upper = jnp.where(k == j + 128, jnp.where(odd == 0, -16.0, 1.0), 0.0)
    spread[...] = (from_word + from_upper).astype(jnp.bfloat16)
    squares[...] = jnp.zeros_like(squares)

    def unpack_chunk(c):
        code_copy(c).wait()
        block_scale = scale_v[:, whole(c)].T
        slot = c % SLOTS
        for b in range(code_v.shape[2] // 128):
            word = code_v[slot, :, 128 * b : 128 * b + 128]
            pair = jnp.concatenate(
                [
                    (word - 136).astype(jnp.float32).astype(jnp.bfloat16),
                    ((word >> 4) - 8).astype(jnp.float32).astype(jnp.bfloat16),
                ],
                axis=1,
            )
            centered = jnp.dot(pair, spread[...], preferred_element_type=jnp.float32)
            for part in range(2):
                col = 256 * b + 128 * part
                q, at = col // quarter, col % quarter
                value = centered[:, 128 * part : 128 * part + 128]
                value = value * block_scale[:, 2 * b + part : 2 * b + part + 1]
                pseudo[q // 2, q % 2, whole(c), at : at + 128] = value.astype(jnp.bfloat16)

        @pl.when(c + SLOTS < count)
        def _():
            code_copy(c + SLOTS).start()

    def square_chunk(c):
        wide = 2 * chunk
        cols = pl.ds(pl.multiple_of(c * wide, wide), wide)
        g = gate_v[:, cols].astype(jnp.float32)
        h = g * jax.nn.sigmoid(g) * up_v[:, cols].astype(jnp.float32)
        hid_t[cols, :] = h.T.astype(jnp.bfloat16)
        for q in range(4):
            grad = jnp.dot(
                hid_t[cols, :], og_v[:, quarter * q : quarter * (q + 1)],
                preferred_element_type=jnp.float32,
            ) * (1.0 / tok_total)
            squares[...] += jnp.sum((grad * grad).reshape(wide // 8, 8, quarter), axis=0)

    def send_sums():
        sums[0] = jnp.full((8, 128), jnp.sum(squares[...]), jnp.float32)
        for step in range(1, shards):
            sum_copy(step).start()

    def pass_chunk(c):
        scatter_x(c).wait_recv()
        mine = pseudo[1 - y, x, first(c)].astype(jnp.float32)
        sa[packed(c)] = (mine + ra[1 - y, packed(c)].astype(jnp.float32)).astype(jnp.bfloat16)
        pass_y(c).start()
        scatter_y(c).wait_recv()
        mine = pseudo[y, 1 - x, second(c)].astype(jnp.float32)
        sb[packed(c)] = (mine + rb[1 - x, packed(c)].astype(jnp.float32)).astype(jnp.bfloat16)
        pass_x(c).start()

    def outer_rows(at, total):
        new_momentum, new_global = outer_update(total * 0.25, mom_v[at], glob_v[at])
        mom_v[at] = new_momentum
        glob_v[at] = new_global
        gbf[y, x, at] = new_global.astype(jnp.bfloat16)

    def outer_chunk(c):
        f32 = jnp.float32
        pass_y(c).wait_recv()
        at, near = first(c), packed(c)
        outer_rows(at, pseudo[y, x, at].astype(f32) + ra[y, near].astype(f32) + r2a[near].astype(f32))
        pass_x(c).wait_recv()
        at = second(c)
        outer_rows(at, pseudo[y, x, at].astype(f32) + rb[x, near].astype(f32) + r2b[near].astype(f32))
        own_x(c, x).start()
        own_y(c, y).start()

    def find_factor():
        for step in range(1, shards):
            sum_copy(step).wait_recv()
        total = sums[0]
        for step in range(1, shards):
            total = total + sums[step]
        root_mean = jnp.sqrt(total / all_entries + 1e-06)
        scale = jnp.minimum(1.0, 0.02 / root_mean) * (0.4 / tok_total)
        factor[...] = jnp.concatenate([scale] * (quarter // 128), axis=1)

    def onward_chunk(c):
        own_y(c, 1 - y).wait_recv()
        onward_x(c, x).start()
        own_x(c, 1 - x).wait_recv()
        onward_y(c, y).start()

    def merge_chunk(c):
        slot = c % 2
        inner_copy(c).wait()

        scatter_x(c).wait_send()
        scatter_y(c).wait_send()
        onward_x(c, 1 - x).wait_recv()
        onward_y(c, 1 - y).wait_recv()
        for q in range(4):
            cols = slice(quarter * q, quarter * (q + 1))
            grad = jnp.dot(hid_t[whole(c), :], og_v[:, cols], preferred_element_type=jnp.float32)
            kept = 0.42 * inner_v[slot, :, cols].astype(jnp.float32)
            kept = kept + 0.5 * gbf[q // 2, q % 2, whole(c)].astype(jnp.float32)
            pseudo[q // 2, q % 2, whole(c)] = (kept - grad * factor[0:1, :]).astype(jnp.bfloat16)

        @pl.when(c + 2 < count)
        def _():
            inner_copy(c + 2).start()

    scale_load.wait()
    unpack_chunk(0)
    pl.semaphore_wait(barrier, shards + 1)
    for load in (gate_load, up_load, og_load, glob_load, mom_load):
        load.start()
    for c in range(min(2, count)):
        inner_copy(c).start()

    merge_lag = max(4 * LAG, LAG + count // 2)

    def step(s, carry):
        @pl.when(s < count)
        def _():
            scatter_x(s).start()
            scatter_y(s).start()

        @pl.when(s + 1 < count)
        def _():
            unpack_chunk(s + 1)

        @pl.when((s >= LAG) & (s < count + LAG))
        def _():
            pass_chunk(s - LAG)

        @pl.when(s == 2 * LAG)
        def _():
            glob_load.wait()
            mom_load.wait()

        @pl.when((s >= 2 * LAG) & (s < count + 2 * LAG))
        def _():
            outer_chunk(s - 2 * LAG)

        @pl.when((s >= 3 * LAG) & (s < count + 3 * LAG))
        def _():
            onward_chunk(s - 3 * LAG)

        @pl.when(s == LAG)
        def _():
            gate_load.wait()
            up_load.wait()
            og_load.wait()

        @pl.when((s >= LAG) & (s < LAG + count // 2))
        def _():
            square_chunk(s - LAG)

        @pl.when(s == LAG + count // 2 - 1)
        def _():
            send_sums()

        @pl.when(s == merge_lag)
        def _():
            find_factor()

        @pl.when(s >= merge_lag)
        def _():
            merge_chunk(s - merge_lag)

        return carry

    lax.fori_loop(0, count + merge_lag, step, 0)

    def drain(c, carry):
        pass_y(c).wait_send()
        pass_x(c).wait_send()
        own_x(c, x).wait_send()
        own_y(c, y).wait_send()
        onward_x(c, x).wait_send()
        onward_y(c, y).wait_send()
        return carry

    lax.fori_loop(0, count, drain, 0)
    for step in range(1, shards):
        sum_copy(step).wait_send()


def write_results(merged_v, glob_v, mom_v, merged_out, glob_out, mom_out, sem):
    rows, quarter = glob_v.shape
    copies = []
    for q in range(4):
        place = merged_out.at[:, pl.ds(quarter * q, quarter)]
        copies.append(pltpu.make_async_copy(merged_v.at[q // 2, q % 2], place, sem.at[q]))
    for index, (held, out) in enumerate(((glob_v, glob_out), (mom_v, mom_out))):
        for part in range(2):
            at = pl.ds(part * (rows // 2), rows // 2)
            copies.append(
                pltpu.make_async_copy(held.at[at], out.at[at], sem.at[4 + 2 * index + part])
            )
    for copy in copies:
        copy.start()
    for copy in copies:
        copy.wait()


def per_device_square(
    gate_pre, up_pre, out_grad, inner_params, global_params, outer_momentum, pair_codes, code_scales
):
    shards = lax.axis_size("fsdp")
    tokens, rows = gate_pre.shape
    width = out_grad.shape[1]
    quarter = width // 4
    chunk = 128
    count = rows // chunk
    bf16, f32 = jnp.bfloat16, jnp.float32
    dma = pltpu.SemaphoreType.DMA
    any_spec = pl.BlockSpec(memory_space=pl.ANY)
    vmem_spec = pl.BlockSpec(memory_space=pltpu.VMEM)
    merged, new_global, new_momentum = pl.pallas_call(
        functools.partial(fused_step, chunk, shards, tokens, rows * shards * width),
        out_shape=(
            pltpu.VMEM((2, 2, rows, quarter), bf16),
            pltpu.VMEM((rows, quarter), f32),
            pltpu.VMEM((rows, quarter), f32),
        ),
        in_specs=[any_spec] * 8,
        out_specs=(vmem_spec,) * 3,
        scratch_shapes=[
            pltpu.VMEM((2, rows // 2, quarter), bf16),
            pltpu.VMEM((2, rows // 2, quarter), bf16),
            pltpu.VMEM((rows // 2, quarter), bf16),
            pltpu.VMEM((rows // 2, quarter), bf16),
            pltpu.VMEM((rows // 2, quarter), bf16),
            pltpu.VMEM((rows // 2, quarter), bf16),
            pltpu.VMEM((2, 2, rows, quarter), bf16),
            pltpu.VMEM((SLOTS, chunk, width // 2), jnp.int32),
            pltpu.VMEM((code_scales.shape[2], rows), f32),
            pltpu.VMEM((tokens, rows), bf16),
            pltpu.VMEM((tokens, rows), bf16),
            pltpu.VMEM((tokens, width), bf16),
            pltpu.VMEM((rows, tokens), bf16),
            pltpu.VMEM((2, chunk, width), bf16),
            pltpu.VMEM((256, 256), bf16),
            pltpu.VMEM((8, quarter), f32),
            pltpu.VMEM((shards, 8, 128), f32),
            pltpu.VMEM((8, quarter), f32),
            dma((8, count)),
            dma((8, count)),
            dma((shards - 1,)),
            dma((shards - 1,)),
            dma((SLOTS,)),
            dma((6,)),
            dma((2,)),
        ],
        compiler_params=pltpu.CompilerParams(
            collective_id=0, has_side_effects=True, vmem_limit_bytes=40 * 1024 * 1024
        ),
        cost_estimate=pl.CostEstimate(
            flops=4 * tokens * rows * width, bytes_accessed=22 * rows * width, transcendentals=0
        ),
    )(
        gate_pre, up_pre, out_grad, inner_params[0], global_params, outer_momentum,
        pair_codes[0], code_scales[0].T,
    )
    merged, new_global, new_momentum = pl.pallas_call(
        write_results,
        out_shape=(
            jax.ShapeDtypeStruct((rows, width), bf16),
            jax.ShapeDtypeStruct((rows, quarter), f32),
            jax.ShapeDtypeStruct((rows, quarter), f32),
        ),
        in_specs=[vmem_spec] * 3,
        out_specs=(any_spec,) * 3,
        scratch_shapes=[dma((8,))],
        compiler_params=pltpu.CompilerParams(vmem_limit_bytes=4 * 1024 * 1024),
        cost_estimate=pl.CostEstimate(
            flops=0, bytes_accessed=4 * rows * width, transcendentals=0
        ),
    )(merged, new_global, new_momentum)
    return (merged[None], new_global, new_momentum)


def per_device(*arrays):
    rows, width = arrays[0].shape[1], arrays[2].shape[1]
    square = lax.axis_size("rep") == 4 and lax.axis_size("fsdp") > 1
    if square and rows % 256 == 0 and width % 1024 == 0 and width // arrays[7].shape[2] == 128:
        return per_device_square(*arrays)
    return per_device_any(*arrays)


def solution(mesh):
    in_specs = (
        P("rep", "fsdp"),
        P("rep", "fsdp"),
        P("rep", None),
        P("rep", "fsdp", None),
        P("fsdp", "rep"),
        P("fsdp", "rep"),
        P("rep", "fsdp", None),
        P("rep", "fsdp", None),
    )
    out_specs = (P("rep", "fsdp", None), P("fsdp", "rep"), P("fsdp", "rep"))
    return jax.shard_map(
        per_device, mesh=mesh, in_specs=in_specs, out_specs=out_specs, check_vma=False
    )
```

```python
import functools
import jax
import jax.numpy as jnp
from jax import lax
from jax.experimental import pallas as pl
from jax.experimental.pallas import tpu as pltpu
from jax.sharding import PartitionSpec as P


def outer_update(mean_delta, momentum, params):
    new_momentum = 0.9 * momentum + mean_delta
    new_global = params - 0.7 * (mean_delta + 0.9 * new_momentum)
    return (new_momentum, new_global)


def unpack(packed, scales):
    lower_code = packed % 16
    upper_code = packed // 16
    unpacked = jnp.stack([lower_code, upper_code], axis=-1).reshape(
        packed.shape[:-1] + (2 * packed.shape[-1],)
    )
    centered = (unpacked - 8).astype(jnp.float32)
    blocks = centered.reshape(packed.shape[:-1] + (scales.shape[-1], -1)) * scales[..., None]
    return blocks.reshape(unpacked.shape).astype(jnp.bfloat16)


def per_device_any(
    gate_pre, up_pre, out_grad, inner_params, global_params, outer_momentum, pair_codes, code_scales
):
    replicas = lax.axis_size("rep")
    tok_total = gate_pre.shape[0]
    unit_rows = gate_pre.shape[1]
    model_width = out_grad.shape[1]
    all_units = unit_rows * lax.axis_size("fsdp")
    gate_f32 = gate_pre.astype(jnp.float32)
    upper = up_pre.astype(jnp.float32)
    sigmoid_gate = jax.nn.sigmoid(gate_f32)
    hidden = (gate_f32 * sigmoid_gate * upper).astype(jnp.bfloat16)
    grads = lax.dot_general(
        hidden, out_grad, (((0,), (0,)), ((), ())), preferred_element_type=jnp.float32
    ) * (1.0 / tok_total)
    square_total = lax.psum(jnp.sum(grads * grads), "fsdp")
    root_mean = jnp.sqrt(square_total / (all_units * model_width) + 1e-06)
    clipped = grads * jnp.minimum(1.0, 0.02 / root_mean)
    pseudo = unpack(pair_codes[0], code_scales[0])
    delta_share = lax.psum_scatter(pseudo, "rep", scatter_dimension=1, tiled=True).astype(
        jnp.float32
    ) * (1.0 / replicas)
    new_momentum, new_global = outer_update(delta_share, outer_momentum, global_params)
    global_bf = lax.all_gather(new_global.astype(jnp.bfloat16), "rep", axis=1, tiled=True).astype(
        jnp.float32
    )
    master = inner_params[0].astype(jnp.float32)
    stepped = master - 0.8 * (clipped + 0.2 * master)
    merged_params = (0.5 * stepped + 0.5 * global_bf).astype(jnp.bfloat16)
    return (merged_params[None], new_global, new_momentum)


SLOTS = 4
PASS_LAG, OUTER_LAG, ONWARD_LAG, MERGE_LAG = 4, 7, 10, 13
WIDE = 256
MESH = pl.DeviceIdType.MESH


def fused_step(
    chunk, shards, tok_total, all_entries,
    gate, up, og, inner, glob, mom, codes, scales,
    pseudo, glob_v, mom_v,
    ra, rb, sa, sb, r2a, r2b, gbf, code_v, scale_v,
    gate_v, up_v, og_v, hid_t, inner_v, base, scale_t, spread, squares, sums, factor,
    send_sem, recv_sem, sum_send, sum_recv, code_sem, load_sem, inner_sem,
):
    rows = glob_v.shape[0]
    quarter = glob_v.shape[1]
    half = chunk // 2
    count = rows // chunk
    rep = lax.axis_index("rep")
    shard = lax.axis_index("fsdp")
    y, x = rep // 2, rep % 2
    x_peer, y_peer = y * 2 + (1 - x), (1 - y) * 2 + x

    def whole(c):
        return pl.ds(pl.multiple_of(c * chunk, chunk), chunk)

    def first(c):
        return pl.ds(pl.multiple_of(c * chunk, half), half)

    def second(c):
        return pl.ds(pl.multiple_of(c * chunk + half, half), half)

    def packed(c):
        return pl.ds(pl.multiple_of(c * half, half), half)

    def remote(src, dst, kind, c, peer):
        return pltpu.make_async_remote_copy(
            src_ref=src, dst_ref=dst, send_sem=send_sem.at[kind, c], recv_sem=recv_sem.at[kind, c],
            device_id=(peer, shard), device_id_type=MESH,
        )

    def scatter_x(c):
        return remote(pseudo.at[:, 1 - x, first(c)], ra.at[:, packed(c)], 0, c, x_peer)

    def scatter_y(c):
        return remote(pseudo.at[1 - y, :, second(c)], rb.at[:, packed(c)], 1, c, y_peer)

    def pass_y(c):
        return remote(sa.at[packed(c)], r2a.at[packed(c)], 2, c, y_peer)

    def pass_x(c):
        return remote(sb.at[packed(c)], r2b.at[packed(c)], 3, c, x_peer)

    def own_x(c, at_x):
        block = gbf.at[y, at_x, whole(c)]
        return remote(block, block, 4, c, x_peer)

    def own_y(c, at_y):
        block = gbf.at[at_y, x, whole(c)]
        return remote(block, block, 5, c, y_peer)

    def onward_x(c, at_x):
        block = gbf.at[1 - y, at_x, first(c)]
        return remote(block, block, 6, c, x_peer)

    def onward_y(c, at_y):
        block = gbf.at[at_y, 1 - x, second(c)]
        return remote(block, block, 7, c, y_peer)

    def sum_copy(step):
        return pltpu.make_async_remote_copy(
            src_ref=sums.at[0], dst_ref=sums.at[step],
            send_sem=sum_send.at[step - 1], recv_sem=sum_recv.at[step - 1],
            device_id=(rep, (shard + step) % shards), device_id_type=MESH,
        )

    def code_copy(c):
        return pltpu.make_async_copy(
            codes.at[whole(c)], code_v.at[c % SLOTS], code_sem.at[c % SLOTS]
        )

    def inner_copy(c):
        return pltpu.make_async_copy(inner.at[whole(c)], inner_v.at[c % 2], inner_sem.at[c % 2])

    scale_load = pltpu.make_async_copy(scales, scale_v, load_sem.at[0])
    gate_load = pltpu.make_async_copy(gate, gate_v, load_sem.at[1])
    up_load = pltpu.make_async_copy(up, up_v, load_sem.at[2])
    og_load = pltpu.make_async_copy(og, og_v, load_sem.at[3])
    glob_load = pltpu.make_async_copy(glob, glob_v, load_sem.at[4])
    mom_load = pltpu.make_async_copy(mom, mom_v, load_sem.at[5])
    code_copy(0).start()
    scale_load.start()
    for c in range(1, min(SLOTS, count)):
        code_copy(c).start()

    barrier = pltpu.get_barrier_semaphore()
    for peer in (x_peer, y_peer):
        pl.semaphore_signal(barrier, inc=1, device_id=(peer, shard), device_id_type=MESH)
    for step in range(1, shards):
        pl.semaphore_signal(
            barrier, inc=1, device_id=(rep, (shard + step) % shards), device_id_type=MESH
        )

    k = lax.broadcasted_iota(jnp.int32, (256, 256), 0)
    n = lax.broadcasted_iota(jnp.int32, (256, 256), 1)
    j, odd = n >> 1, n & 1
    from_word = jnp.where((k == j) & (odd == 0), 1.0, 0.0)
    from_upper = jnp.where(k == j + 128, jnp.where(odd == 0, -16.0, 1.0), 0.0)
    spread[...] = (from_word + from_upper).astype(jnp.bfloat16)
    squares[...] = jnp.zeros_like(squares)

    def unpack_chunk(c):
        code_copy(c).wait()
        share = 128 // chunk

        @pl.when(c % share == 0)
        def _():
            lanes = pl.ds(pl.multiple_of(c // share * 128, 128), 128)
            scale_t[...] = scale_v[:, lanes].T

        block_scale = scale_t[pl.ds(pl.multiple_of(c % share * chunk, chunk), chunk), :]
        slot = c % SLOTS
        for b in range(code_v.shape[2] // 128):
            word = code_v[slot, :, 128 * b : 128 * b + 128]
            pair = jnp.concatenate(
                [
                    (word - 136).astype(jnp.float32).astype(jnp.bfloat16),
                    ((word >> 4) - 8).astype(jnp.float32).astype(jnp.bfloat16),
                ],
                axis=1,
            )
            centered = jnp.dot(pair, spread[...], preferred_element_type=jnp.float32)
            for part in range(2):
                col = 256 * b + 128 * part
                q, at = col // quarter, col % quarter
                value = centered[:, 128 * part : 128 * part + 128]
                value = value * block_scale[:, 2 * b + part : 2 * b + part + 1]
                pseudo[q // 2, q % 2, whole(c), at : at + 128] = value.astype(jnp.bfloat16)

        @pl.when(c + SLOTS < count)
        def _():
            code_copy(c + SLOTS).start()

    def square_chunk(c):
        cols = pl.ds(pl.multiple_of(c * WIDE, WIDE), WIDE)
        g = gate_v[:, cols].astype(jnp.float32)
        h = g * jax.nn.sigmoid(g) * up_v[:, cols].astype(jnp.float32)
        hid_t[cols, :] = h.T.astype(jnp.bfloat16)
        for q in range(4):
            grad = jnp.dot(
                hid_t[cols, :], og_v[:, quarter * q : quarter * (q + 1)],
                preferred_element_type=jnp.float32,
            ) * (1.0 / tok_total)
            squares[...] += jnp.sum((grad * grad).reshape(WIDE // 8, 8, quarter), axis=0)

    def send_sums():
        sums[0] = jnp.full((8, 128), jnp.sum(squares[...]), jnp.float32)
        for step in range(1, shards):
            sum_copy(step).start()

    def pass_chunk(c):
        scatter_x(c).wait_recv()
        mine = pseudo[1 - y, x, first(c)].astype(jnp.float32)
        sa[packed(c)] = (mine + ra[1 - y, packed(c)].astype(jnp.float32)).astype(jnp.bfloat16)
        pass_y(c).start()
        scatter_y(c).wait_recv()
        mine = pseudo[y, 1 - x, second(c)].astype(jnp.float32)
        sb[packed(c)] = (mine + rb[1 - x, packed(c)].astype(jnp.float32)).astype(jnp.bfloat16)
        pass_x(c).start()

    def outer_rows(at, total):
        new_momentum, new_global = outer_update(total * 0.25, mom_v[at], glob_v[at])
        mom_v[at] = new_momentum
        glob_v[at] = new_global
        gbf[y, x, at] = new_global.astype(jnp.bfloat16)

    def outer_chunk(c):
        f32 = jnp.float32
        pass_y(c).wait_recv()
        at, near = first(c), packed(c)
        outer_rows(at, pseudo[y, x, at].astype(f32) + ra[y, near].astype(f32) + r2a[near].astype(f32))
        pass_x(c).wait_recv()
        at = second(c)
        outer_rows(at, pseudo[y, x, at].astype(f32) + rb[x, near].astype(f32) + r2b[near].astype(f32))
        own_x(c, x).start()
        own_y(c, y).start()

    def find_factor():
        for step in range(1, shards):
            sum_copy(step).wait_recv()
        total = sums[0]
        for step in range(1, shards):
            total = total + sums[step]
        root_mean = jnp.sqrt(total / all_entries + 1e-06)
        scale = jnp.minimum(1.0, 0.02 / root_mean) * (0.4 / tok_total)
        factor[...] = jnp.concatenate([scale] * (quarter // 128), axis=1)

    def onward_chunk(c):
        own_y(c, 1 - y).wait_recv()
        onward_x(c, x).start()
        own_x(c, 1 - x).wait_recv()
        onward_y(c, y).start()

    def merge_chunk(c):
        slot = c % 2
        inner_copy(c).wait()

        for q in range(4):
            cols = slice(quarter * q, quarter * (q + 1))
            grad = jnp.dot(hid_t[whole(c), :], og_v[:, cols], preferred_element_type=jnp.float32)
            kept = 0.42 * inner_v[slot, :, cols].astype(jnp.float32)
            base[:, cols] = kept - grad * factor[0:1, :]

        @pl.when(c + 2 < count)
        def _():
            inner_copy(c + 2).start()

        scatter_x(c).wait_send()
        scatter_y(c).wait_send()
        onward_x(c, 1 - x).wait_recv()
        onward_y(c, 1 - y).wait_recv()
        for q in range(4):
            arrived = gbf[q // 2, q % 2, whole(c)].astype(jnp.float32)
            kept = base[:, quarter * q : quarter * (q + 1)] + 0.5 * arrived
            pseudo[q // 2, q % 2, whole(c)] = kept.astype(jnp.bfloat16)

    scale_load.wait()
    unpack_chunk(0)
    pl.semaphore_wait(barrier, shards + 1)
    for load in (gate_load, up_load, og_load, glob_load, mom_load):
        load.start()
    for c in range(min(2, count)):
        inner_copy(c).start()

    merge_lag = max(MERGE_LAG, PASS_LAG + rows // WIDE)

    def step(s, carry):
        @pl.when(s < count)
        def _():
            scatter_x(s).start()
            scatter_y(s).start()

        @pl.when(s + 1 < count)
        def _():
            unpack_chunk(s + 1)

        @pl.when((s >= PASS_LAG) & (s < count + PASS_LAG))
        def _():
            pass_chunk(s - PASS_LAG)

        @pl.when(s == OUTER_LAG)
        def _():
            glob_load.wait()
            mom_load.wait()

        @pl.when((s >= OUTER_LAG) & (s < count + OUTER_LAG))
        def _():
            outer_chunk(s - OUTER_LAG)

        @pl.when((s >= ONWARD_LAG) & (s < count + ONWARD_LAG))
        def _():
            onward_chunk(s - ONWARD_LAG)

        @pl.when(s == PASS_LAG)
        def _():
            gate_load.wait()
            up_load.wait()
            og_load.wait()

        @pl.when((s >= PASS_LAG) & (s < PASS_LAG + rows // WIDE))
        def _():
            square_chunk(s - PASS_LAG)

        @pl.when(s == PASS_LAG + rows // WIDE - 1)
        def _():
            send_sums()

        @pl.when(s == merge_lag)
        def _():
            find_factor()

        @pl.when(s >= merge_lag)
        def _():
            merge_chunk(s - merge_lag)

        return carry

    lax.fori_loop(0, count + merge_lag, step, 0)

    def drain(c, carry):
        pass_y(c).wait_send()
        pass_x(c).wait_send()
        own_x(c, x).wait_send()
        own_y(c, y).wait_send()
        onward_x(c, x).wait_send()
        onward_y(c, y).wait_send()
        return carry

    lax.fori_loop(0, count, drain, 0)
    for step in range(1, shards):
        sum_copy(step).wait_send()


def write_results(merged_v, glob_v, mom_v, merged_out, glob_out, mom_out, sem):
    rows, quarter = glob_v.shape
    copies = []
    for q in range(4):
        for part in range(2):
            at = pl.ds(part * (rows // 2), rows // 2)
            place = merged_out.at[at, pl.ds(quarter * q, quarter)]
            copies.append(
                pltpu.make_async_copy(merged_v.at[q // 2, q % 2, at], place, sem.at[len(copies)])
            )
    for held, out in ((glob_v, glob_out), (mom_v, mom_out)):
        for part in range(4):
            at = pl.ds(part * (rows // 4), rows // 4)
            copies.append(pltpu.make_async_copy(held.at[at], out.at[at], sem.at[len(copies)]))
    for copy in copies:
        copy.start()
    for copy in copies:
        copy.wait()


def per_device_square(
    gate_pre, up_pre, out_grad, inner_params, global_params, outer_momentum, pair_codes, code_scales
):
    shards = lax.axis_size("fsdp")
    tokens, rows = gate_pre.shape
    width = out_grad.shape[1]
    quarter = width // 4
    chunk = 64
    count = rows // chunk
    bf16, f32 = jnp.bfloat16, jnp.float32
    dma = pltpu.SemaphoreType.DMA
    any_spec = pl.BlockSpec(memory_space=pl.ANY)
    vmem_spec = pl.BlockSpec(memory_space=pltpu.VMEM)
    merged, new_global, new_momentum = pl.pallas_call(
        functools.partial(fused_step, chunk, shards, tokens, rows * shards * width),
        out_shape=(
            pltpu.VMEM((2, 2, rows, quarter), bf16),
            pltpu.VMEM((rows, quarter), f32),
            pltpu.VMEM((rows, quarter), f32),
        ),
        in_specs=[any_spec] * 8,
        out_specs=(vmem_spec,) * 3,
        scratch_shapes=[
            pltpu.VMEM((2, rows // 2, quarter), bf16),
            pltpu.VMEM((2, rows // 2, quarter), bf16),
            pltpu.VMEM((rows // 2, quarter), bf16),
            pltpu.VMEM((rows // 2, quarter), bf16),
            pltpu.VMEM((rows // 2, quarter), bf16),
            pltpu.VMEM((rows // 2, quarter), bf16),
            pltpu.VMEM((2, 2, rows, quarter), bf16),
            pltpu.VMEM((SLOTS, chunk, width // 2), jnp.int32),
            pltpu.VMEM((code_scales.shape[2], rows), f32),
            pltpu.VMEM((tokens, rows), bf16),
            pltpu.VMEM((tokens, rows), bf16),
            pltpu.VMEM((tokens, width), bf16),
            pltpu.VMEM((rows, tokens), bf16),
            pltpu.VMEM((2, chunk, width), bf16),
            pltpu.VMEM((chunk, width), f32),
            pltpu.VMEM((128, code_scales.shape[2]), f32),
            pltpu.VMEM((256, 256), bf16),
            pltpu.VMEM((8, quarter), f32),
            pltpu.VMEM((shards, 8, 128), f32),
            pltpu.VMEM((8, quarter), f32),
            dma((8, count)),
            dma((8, count)),
            dma((shards - 1,)),
            dma((shards - 1,)),
            dma((SLOTS,)),
            dma((6,)),
            dma((2,)),
        ],
        compiler_params=pltpu.CompilerParams(
            collective_id=0, has_side_effects=True, vmem_limit_bytes=40 * 1024 * 1024
        ),
        cost_estimate=pl.CostEstimate(
            flops=4 * tokens * rows * width, bytes_accessed=22 * rows * width, transcendentals=0
        ),
    )(
        gate_pre, up_pre, out_grad, inner_params[0], global_params, outer_momentum,
        pair_codes[0], code_scales[0].T,
    )
    merged, new_global, new_momentum = pl.pallas_call(
        write_results,
        out_shape=(
            jax.ShapeDtypeStruct((rows, width), bf16),
            jax.ShapeDtypeStruct((rows, quarter), f32),
            jax.ShapeDtypeStruct((rows, quarter), f32),
        ),
        in_specs=[vmem_spec] * 3,
        out_specs=(any_spec,) * 3,
        scratch_shapes=[dma((16,))],
        compiler_params=pltpu.CompilerParams(vmem_limit_bytes=4 * 1024 * 1024),
        cost_estimate=pl.CostEstimate(
            flops=0, bytes_accessed=4 * rows * width, transcendentals=0
        ),
    )(merged, new_global, new_momentum)
    return (merged[None], new_global, new_momentum)


def per_device(*arrays):
    rows, width = arrays[0].shape[1], arrays[2].shape[1]
    square = lax.axis_size("rep") == 4 and lax.axis_size("fsdp") > 1
    if square and rows % WIDE == 0 and width % 1024 == 0 and width // arrays[7].shape[2] == 128:
        return per_device_square(*arrays)
    return per_device_any(*arrays)


def solution(mesh):
    in_specs = (
        P("rep", "fsdp"),
        P("rep", "fsdp"),
        P("rep", None),
        P("rep", "fsdp", None),
        P("fsdp", "rep"),
        P("fsdp", "rep"),
        P("rep", "fsdp", None),
        P("rep", "fsdp", None),
    )
    out_specs = (P("rep", "fsdp", None), P("fsdp", "rep"), P("fsdp", "rep"))
    return jax.shard_map(
        per_device, mesh=mesh, in_specs=in_specs, out_specs=out_specs, check_vma=False
    )
```

```python
import functools
import jax
import jax.numpy as jnp
from jax import lax
from jax.experimental import pallas as pl
from jax.experimental.pallas import tpu as pltpu
from jax.sharding import PartitionSpec as P


def outer_update(mean_delta, momentum, params):
    new_momentum = 0.9 * momentum + mean_delta
    new_global = params - 0.7 * (mean_delta + 0.9 * new_momentum)
    return (new_momentum, new_global)


def unpack(packed, scales):
    lower_code = packed % 16
    upper_code = packed // 16
    unpacked = jnp.stack([lower_code, upper_code], axis=-1).reshape(
        packed.shape[:-1] + (2 * packed.shape[-1],)
    )
    centered = (unpacked - 8).astype(jnp.float32)
    blocks = centered.reshape(packed.shape[:-1] + (scales.shape[-1], -1)) * scales[..., None]
    return blocks.reshape(unpacked.shape).astype(jnp.bfloat16)


def per_device_any(
    gate_pre, up_pre, out_grad, inner_params, global_params, outer_momentum, pair_codes, code_scales
):
    replicas = lax.axis_size("rep")
    tok_total = gate_pre.shape[0]
    unit_rows = gate_pre.shape[1]
    model_width = out_grad.shape[1]
    all_units = unit_rows * lax.axis_size("fsdp")
    gate_f32 = gate_pre.astype(jnp.float32)
    upper = up_pre.astype(jnp.float32)
    sigmoid_gate = jax.nn.sigmoid(gate_f32)
    hidden = (gate_f32 * sigmoid_gate * upper).astype(jnp.bfloat16)
    grads = lax.dot_general(
        hidden, out_grad, (((0,), (0,)), ((), ())), preferred_element_type=jnp.float32
    ) * (1.0 / tok_total)
    square_total = lax.psum(jnp.sum(grads * grads), "fsdp")
    root_mean = jnp.sqrt(square_total / (all_units * model_width) + 1e-06)
    clipped = grads * jnp.minimum(1.0, 0.02 / root_mean)
    pseudo = unpack(pair_codes[0], code_scales[0])
    delta_share = lax.psum_scatter(pseudo, "rep", scatter_dimension=1, tiled=True).astype(
        jnp.float32
    ) * (1.0 / replicas)
    new_momentum, new_global = outer_update(delta_share, outer_momentum, global_params)
    global_bf = lax.all_gather(new_global.astype(jnp.bfloat16), "rep", axis=1, tiled=True).astype(
        jnp.float32
    )
    master = inner_params[0].astype(jnp.float32)
    stepped = master - 0.8 * (clipped + 0.2 * master)
    merged_params = (0.5 * stepped + 0.5 * global_bf).astype(jnp.bfloat16)
    return (merged_params[None], new_global, new_momentum)


SLOTS = 4
LAG = 2
MESH = pl.DeviceIdType.MESH


def fused_step(
    chunk, shards, tok_total, all_entries,
    gate, up, og, inner, glob, mom, codes, scales,
    pseudo, glob_v, mom_v,
    ra, rb, sa, sb, r2a, r2b, gbf, code_v, scale_v,
    gate_v, up_v, og_v, hid_t, inner_v, base, spread, squares, sums, factor,
    send_sem, recv_sem, sum_send, sum_recv, code_sem, load_sem, inner_sem, ready, opened,
):
    rows = glob_v.shape[0]
    quarter = glob_v.shape[1]
    half = chunk // 2
    count = rows // chunk
    rep = lax.axis_index("rep")
    shard = lax.axis_index("fsdp")
    y, x = rep // 2, rep % 2
    x_peer, y_peer = y * 2 + (1 - x), (1 - y) * 2 + x

    def whole(c):
        return pl.ds(pl.multiple_of(c * chunk, chunk), chunk)

    def first(c):
        return pl.ds(pl.multiple_of(c * chunk, half), half)

    def second(c):
        return pl.ds(pl.multiple_of(c * chunk + half, half), half)

    def packed(c):
        return pl.ds(pl.multiple_of(c * half, half), half)

    def remote(src, dst, kind, c, peer):
        return pltpu.make_async_remote_copy(
            src_ref=src, dst_ref=dst, send_sem=send_sem.at[kind, c], recv_sem=recv_sem.at[kind, c],
            device_id=(peer, shard), device_id_type=MESH,
        )

    def scatter_x(c):
        return remote(pseudo.at[:, 1 - x, first(c)], ra.at[:, packed(c)], 0, c, x_peer)

    def scatter_y(c):
        return remote(pseudo.at[1 - y, :, second(c)], rb.at[:, packed(c)], 1, c, y_peer)

    def pass_y(c):
        return remote(sa.at[packed(c)], r2a.at[packed(c)], 2, c, y_peer)

    def pass_x(c):
        return remote(sb.at[packed(c)], r2b.at[packed(c)], 3, c, x_peer)

    def own_x(c, at_x):
        block = gbf.at[y, at_x, whole(c)]
        return remote(block, block, 4, c, x_peer)

    def own_y(c, at_y):
        block = gbf.at[at_y, x, whole(c)]
        return remote(block, block, 5, c, y_peer)

    def onward_x(c, at_x):
        block = gbf.at[1 - y, at_x, first(c)]
        return remote(block, block, 6, c, x_peer)

    def onward_y(c, at_y):
        block = gbf.at[at_y, 1 - x, second(c)]
        return remote(block, block, 7, c, y_peer)

    def sum_copy(step):
        return pltpu.make_async_remote_copy(
            src_ref=sums.at[0], dst_ref=sums.at[step],
            send_sem=sum_send.at[step - 1], recv_sem=sum_recv.at[step - 1],
            device_id=(rep, (shard + step) % shards), device_id_type=MESH,
        )

    def code_copy(c):
        return pltpu.make_async_copy(
            codes.at[whole(c)], code_v.at[c % SLOTS], code_sem.at[c % SLOTS]
        )

    def inner_copy(c):
        return pltpu.make_async_copy(inner.at[whole(c)], inner_v.at[c % 2], inner_sem.at[c % 2])

    scale_load = pltpu.make_async_copy(scales, scale_v, load_sem.at[0])
    gate_load = pltpu.make_async_copy(gate, gate_v, load_sem.at[1])
    up_load = pltpu.make_async_copy(up, up_v, load_sem.at[2])
    og_load = pltpu.make_async_copy(og, og_v, load_sem.at[3])
    glob_load = pltpu.make_async_copy(glob, glob_v, load_sem.at[4])
    mom_load = pltpu.make_async_copy(mom, mom_v, load_sem.at[5])
    code_copy(0).start()
    scale_load.start()
    for c in range(1, min(SLOTS, count)):
        code_copy(c).start()

    barrier = pltpu.get_barrier_semaphore()

    def signal(semaphore, peer, at_shard):
        pl.semaphore_signal(semaphore, inc=1, device_id=(peer, at_shard), device_id_type=MESH)

    @pl.when(rep == 0)
    def _():
        for peer in (1, 2, 3):
            signal(barrier, peer, shard)

    @pl.when(rep == 3)
    def _():
        for peer in (1, 2):
            signal(barrier, peer, shard)

    def enter():
        @pl.when((rep == 1) | (rep == 2))
        def _():
            pl.semaphore_wait(barrier, 2)
            for peer in (0, 3):
                signal(ready, peer, shard)

        @pl.when(rep == 3)
        def _():
            pl.semaphore_wait(barrier, 1)
            signal(ready, 0, shard)
            pl.semaphore_wait(ready, 2)

        @pl.when(rep == 0)
        def _():
            pl.semaphore_wait(ready, 3)
            for step in range(1, shards):
                signal(barrier, 0, (shard + step) % shards)

    def enter_shards():
        @pl.when(rep == 0)
        def _():
            pl.semaphore_wait(barrier, shards - 1)
            for peer in (1, 2, 3):
                signal(opened, peer, shard)

        @pl.when(rep > 0)
        def _():
            pl.semaphore_wait(opened, 1)

    k = lax.broadcasted_iota(jnp.int32, (256, 256), 0)
    n = lax.broadcasted_iota(jnp.int32, (256, 256), 1)
    j, odd = n >> 1, n & 1
    from_word = jnp.where((k == j) & (odd == 0), 1.0, 0.0)
    from_upper = jnp.where(k == j + 128, jnp.where(odd == 0, -16.0, 1.0), 0.0)
    spread[...] = (from_word + from_upper).astype(jnp.bfloat16)
    squares[...] = jnp.zeros_like(squares)

    def unpack_chunk(c):
        code_copy(c).wait()
        block_scale = scale_v[:, whole(c)].T
        slot = c % SLOTS
        for b in range(code_v.shape[2] // 128):
            word = code_v[slot, :, 128 * b : 128 * b + 128]
            pair = jnp.concatenate(
                [
                    (word - 136).astype(jnp.float32).astype(jnp.bfloat16),
                    ((word >> 4) - 8).astype(jnp.float32).astype(jnp.bfloat16),
                ],
                axis=1,
            )
            centered = jnp.dot(pair, spread[...], preferred_element_type=jnp.float32)
            for part in range(2):
                col = 256 * b + 128 * part
                q, at = col // quarter, col % quarter
                value = centered[:, 128 * part : 128 * part + 128]
                value = value * block_scale[:, 2 * b + part : 2 * b + part + 1]
                pseudo[q // 2, q % 2, whole(c), at : at + 128] = value.astype(jnp.bfloat16)

        @pl.when(c + SLOTS < count)
        def _():
            code_copy(c + SLOTS).start()

    def square_chunk(c):
        wide = 2 * chunk
        cols = pl.ds(pl.multiple_of(c * wide, wide), wide)
        g = gate_v[:, cols].astype(jnp.float32)
        h = g * jax.nn.sigmoid(g) * up_v[:, cols].astype(jnp.float32)
        hid_t[cols, :] = h.T.astype(jnp.bfloat16)
        for q in range(4):
            grad = jnp.dot(
                hid_t[cols, :], og_v[:, quarter * q : quarter * (q + 1)],
                preferred_element_type=jnp.float32,
            ) * (1.0 / tok_total)
            squares[...] += jnp.sum((grad * grad).reshape(wide // 8, 8, quarter), axis=0)

    def send_sums():
        enter_shards()
        sums[0] = jnp.full((8, 128), jnp.sum(squares[...]), jnp.float32)
        for step in range(1, shards):
            sum_copy(step).start()

    def pass_chunk(c):
        scatter_x(c).wait_recv()
        mine = pseudo[1 - y, x, first(c)].astype(jnp.float32)
        sa[packed(c)] = (mine + ra[1 - y, packed(c)].astype(jnp.float32)).astype(jnp.bfloat16)
        pass_y(c).start()
        scatter_y(c).wait_recv()
        mine = pseudo[y, 1 - x, second(c)].astype(jnp.float32)
        sb[packed(c)] = (mine + rb[1 - x, packed(c)].astype(jnp.float32)).astype(jnp.bfloat16)
        pass_x(c).start()

    def outer_rows(at, total):
        new_momentum, new_global = outer_update(total * 0.25, mom_v[at], glob_v[at])
        mom_v[at] = new_momentum
        glob_v[at] = new_global
        gbf[y, x, at] = new_global.astype(jnp.bfloat16)

    def outer_chunk(c):
        f32 = jnp.float32
        pass_y(c).wait_recv()
        at, near = first(c), packed(c)
        outer_rows(at, pseudo[y, x, at].astype(f32) + ra[y, near].astype(f32) + r2a[near].astype(f32))
        pass_x(c).wait_recv()
        at = second(c)
        outer_rows(at, pseudo[y, x, at].astype(f32) + rb[x, near].astype(f32) + r2b[near].astype(f32))
        own_x(c, x).start()
        own_y(c, y).start()

    def find_factor():
        for step in range(1, shards):
            sum_copy(step).wait_recv()
        total = sums[0]
        for step in range(1, shards):
            total = total + sums[step]
        root_mean = jnp.sqrt(total / all_entries + 1e-06)
        scale = jnp.minimum(1.0, 0.02 / root_mean) * (0.4 / tok_total)
        factor[...] = jnp.concatenate([scale] * (quarter // 128), axis=1)

    def onward_chunk(c):
        own_y(c, 1 - y).wait_recv()
        onward_x(c, x).start()
        own_x(c, 1 - x).wait_recv()
        onward_y(c, y).start()

    def merge_chunk(c):
        slot = c % 2
        inner_copy(c).wait()

        for q in range(4):
            cols = slice(quarter * q, quarter * (q + 1))
            grad = jnp.dot(hid_t[whole(c), :], og_v[:, cols], preferred_element_type=jnp.float32)
            kept = 0.42 * inner_v[slot, :, cols].astype(jnp.float32)
            base[:, cols] = kept - grad * factor[0:1, :]

        @pl.when(c + 2 < count)
        def _():
            inner_copy(c + 2).start()

        scatter_x(c).wait_send()
        scatter_y(c).wait_send()
        onward_x(c, 1 - x).wait_recv()
        onward_y(c, 1 - y).wait_recv()
        for q in range(4):
            arrived = gbf[q // 2, q % 2, whole(c)].astype(jnp.float32)
            kept = base[:, quarter * q : quarter * (q + 1)] + 0.5 * arrived
            pseudo[q // 2, q % 2, whole(c)] = kept.astype(jnp.bfloat16)

    scale_load.wait()
    unpack_chunk(0)
    enter()
    for load in (gate_load, up_load, og_load, glob_load, mom_load):
        load.start()
    for c in range(min(2, count)):
        inner_copy(c).start()

    merge_lag = max(4 * LAG, LAG + count // 2)

    def step(s, carry):
        @pl.when(s < count)
        def _():
            scatter_x(s).start()
            scatter_y(s).start()

        @pl.when(s + 1 < count)
        def _():
            unpack_chunk(s + 1)

        @pl.when((s >= LAG) & (s < count + LAG))
        def _():
            pass_chunk(s - LAG)

        @pl.when(s == 2 * LAG)
        def _():
            glob_load.wait()
            mom_load.wait()

        @pl.when((s >= 2 * LAG) & (s < count + 2 * LAG))
        def _():
            outer_chunk(s - 2 * LAG)

        @pl.when((s >= 3 * LAG) & (s < count + 3 * LAG))
        def _():
            onward_chunk(s - 3 * LAG)

        @pl.when(s == LAG)
        def _():
            gate_load.wait()
            up_load.wait()
            og_load.wait()

        @pl.when((s >= LAG) & (s < LAG + count // 2))
        def _():
            square_chunk(s - LAG)

        @pl.when(s == LAG + count // 2 - 1)
        def _():
            send_sums()

        @pl.when(s == merge_lag)
        def _():
            find_factor()

        @pl.when(s >= merge_lag)
        def _():
            merge_chunk(s - merge_lag)

        return carry

    lax.fori_loop(0, count + merge_lag, step, 0)

    def drain(c, carry):
        pass_y(c).wait_send()
        pass_x(c).wait_send()
        own_x(c, x).wait_send()
        own_y(c, y).wait_send()
        onward_x(c, x).wait_send()
        onward_y(c, y).wait_send()
        return carry

    lax.fori_loop(0, count, drain, 0)
    for step in range(1, shards):
        sum_copy(step).wait_send()


def write_results(merged_v, glob_v, mom_v, merged_out, glob_out, mom_out, sem):
    rows, quarter = glob_v.shape
    copies = []
    for q in range(4):
        place = merged_out.at[:, pl.ds(quarter * q, quarter)]
        copies.append(pltpu.make_async_copy(merged_v.at[q // 2, q % 2], place, sem.at[q]))
    for index, (held, out) in enumerate(((glob_v, glob_out), (mom_v, mom_out))):
        for part in range(2):
            at = pl.ds(part * (rows // 2), rows // 2)
            copies.append(
                pltpu.make_async_copy(held.at[at], out.at[at], sem.at[4 + 2 * index + part])
            )
    for copy in copies:
        copy.start()
    for copy in copies:
        copy.wait()


def per_device_square(
    gate_pre, up_pre, out_grad, inner_params, global_params, outer_momentum, pair_codes, code_scales
):
    shards = lax.axis_size("fsdp")
    tokens, rows = gate_pre.shape
    width = out_grad.shape[1]
    quarter = width // 4
    chunk = 128
    count = rows // chunk
    bf16, f32 = jnp.bfloat16, jnp.float32
    dma = pltpu.SemaphoreType.DMA
    any_spec = pl.BlockSpec(memory_space=pl.ANY)
    vmem_spec = pl.BlockSpec(memory_space=pltpu.VMEM)
    merged, new_global, new_momentum = pl.pallas_call(
        functools.partial(fused_step, chunk, shards, tokens, rows * shards * width),
        out_shape=(
            pltpu.VMEM((2, 2, rows, quarter), bf16),
            pltpu.VMEM((rows, quarter), f32),
            pltpu.VMEM((rows, quarter), f32),
        ),
        in_specs=[any_spec] * 8,
        out_specs=(vmem_spec,) * 3,
        scratch_shapes=[
            pltpu.VMEM((2, rows // 2, quarter), bf16),
            pltpu.VMEM((2, rows // 2, quarter), bf16),
            pltpu.VMEM((rows // 2, quarter), bf16),
            pltpu.VMEM((rows // 2, quarter), bf16),
            pltpu.VMEM((rows // 2, quarter), bf16),
            pltpu.VMEM((rows // 2, quarter), bf16),
            pltpu.VMEM((2, 2, rows, quarter), bf16),
            pltpu.VMEM((SLOTS, chunk, width // 2), jnp.int32),
            pltpu.VMEM((code_scales.shape[2], rows), f32),
            pltpu.VMEM((tokens, rows), bf16),
            pltpu.VMEM((tokens, rows), bf16),
            pltpu.VMEM((tokens, width), bf16),
            pltpu.VMEM((rows, tokens), bf16),
            pltpu.VMEM((2, chunk, width), bf16),
            pltpu.VMEM((chunk, width), f32),
            pltpu.VMEM((256, 256), bf16),
            pltpu.VMEM((8, quarter), f32),
            pltpu.VMEM((shards, 8, 128), f32),
            pltpu.VMEM((8, quarter), f32),
            dma((8, count)),
            dma((8, count)),
            dma((shards - 1,)),
            dma((shards - 1,)),
            dma((SLOTS,)),
            dma((6,)),
            dma((2,)),
            pltpu.SemaphoreType.REGULAR,
            pltpu.SemaphoreType.REGULAR,
        ],
        compiler_params=pltpu.CompilerParams(
            collective_id=0, has_side_effects=True, vmem_limit_bytes=40 * 1024 * 1024
        ),
        cost_estimate=pl.CostEstimate(
            flops=4 * tokens * rows * width, bytes_accessed=22 * rows * width, transcendentals=0
        ),
    )(
        gate_pre, up_pre, out_grad, inner_params[0], global_params, outer_momentum,
        pair_codes[0], code_scales[0].T,
    )
    merged, new_global, new_momentum = pl.pallas_call(
        write_results,
        out_shape=(
            jax.ShapeDtypeStruct((rows, width), bf16),
            jax.ShapeDtypeStruct((rows, quarter), f32),
            jax.ShapeDtypeStruct((rows, quarter), f32),
        ),
        in_specs=[vmem_spec] * 3,
        out_specs=(any_spec,) * 3,
        scratch_shapes=[dma((8,))],
        compiler_params=pltpu.CompilerParams(vmem_limit_bytes=4 * 1024 * 1024),
        cost_estimate=pl.CostEstimate(
            flops=0, bytes_accessed=4 * rows * width, transcendentals=0
        ),
    )(merged, new_global, new_momentum)
    return (merged[None], new_global, new_momentum)


def per_device(*arrays):
    rows, width = arrays[0].shape[1], arrays[2].shape[1]
    square = lax.axis_size("rep") == 4 and lax.axis_size("fsdp") > 1
    if square and rows % 256 == 0 and width % 1024 == 0 and width // arrays[7].shape[2] == 128:
        return per_device_square(*arrays)
    return per_device_any(*arrays)


def solution(mesh):
    in_specs = (
        P("rep", "fsdp"),
        P("rep", "fsdp"),
        P("rep", None),
        P("rep", "fsdp", None),
        P("fsdp", "rep"),
        P("fsdp", "rep"),
        P("rep", "fsdp", None),
        P("rep", "fsdp", None),
    )
    out_specs = (P("rep", "fsdp", None), P("fsdp", "rep"), P("fsdp", "rep"))
    return jax.shard_map(
        per_device, mesh=mesh, in_specs=in_specs, out_specs=out_specs, check_vma=False
    )
```

```python
import functools
import jax
import jax.numpy as jnp
from jax import lax
from jax.experimental import pallas as pl
from jax.experimental.pallas import tpu as pltpu
from jax.sharding import PartitionSpec as P


def outer_update(mean_delta, momentum, params):
    new_momentum = 0.9 * momentum + mean_delta
    new_global = params - 0.7 * (mean_delta + 0.9 * new_momentum)
    return (new_momentum, new_global)


def unpack(packed, scales):
    lower_code = packed % 16
    upper_code = packed // 16
    unpacked = jnp.stack([lower_code, upper_code], axis=-1).reshape(
        packed.shape[:-1] + (2 * packed.shape[-1],)
    )
    centered = (unpacked - 8).astype(jnp.float32)
    blocks = centered.reshape(packed.shape[:-1] + (scales.shape[-1], -1)) * scales[..., None]
    return blocks.reshape(unpacked.shape).astype(jnp.bfloat16)


def per_device_any(
    gate_pre, up_pre, out_grad, inner_params, global_params, outer_momentum, pair_codes, code_scales
):
    replicas = lax.axis_size("rep")
    tok_total = gate_pre.shape[0]
    unit_rows = gate_pre.shape[1]
    model_width = out_grad.shape[1]
    all_units = unit_rows * lax.axis_size("fsdp")
    gate_f32 = gate_pre.astype(jnp.float32)
    upper = up_pre.astype(jnp.float32)
    sigmoid_gate = jax.nn.sigmoid(gate_f32)
    hidden = (gate_f32 * sigmoid_gate * upper).astype(jnp.bfloat16)
    grads = lax.dot_general(
        hidden, out_grad, (((0,), (0,)), ((), ())), preferred_element_type=jnp.float32
    ) * (1.0 / tok_total)
    square_total = lax.psum(jnp.sum(grads * grads), "fsdp")
    root_mean = jnp.sqrt(square_total / (all_units * model_width) + 1e-06)
    clipped = grads * jnp.minimum(1.0, 0.02 / root_mean)
    pseudo = unpack(pair_codes[0], code_scales[0])
    delta_share = lax.psum_scatter(pseudo, "rep", scatter_dimension=1, tiled=True).astype(
        jnp.float32
    ) * (1.0 / replicas)
    new_momentum, new_global = outer_update(delta_share, outer_momentum, global_params)
    global_bf = lax.all_gather(new_global.astype(jnp.bfloat16), "rep", axis=1, tiled=True).astype(
        jnp.float32
    )
    master = inner_params[0].astype(jnp.float32)
    stepped = master - 0.8 * (clipped + 0.2 * master)
    merged_params = (0.5 * stepped + 0.5 * global_bf).astype(jnp.bfloat16)
    return (merged_params[None], new_global, new_momentum)


SLOTS = 4
LAG = 2
MESH = pl.DeviceIdType.MESH


def fused_step(
    chunk, shards, tok_total, all_entries,
    gate, up, og, inner, glob, mom, codes, scales,
    pseudo, glob_v, mom_v,
    ra, rb, sa, sb, r2a, r2b, gbf, code_v, scale_v,
    gate_v, up_v, og_v, hid_t, inner_v, base, spread, squares, sums, factor,
    send_sem, recv_sem, sum_send, sum_recv, code_sem, load_sem, inner_sem, ready, opened,
):
    rows = glob_v.shape[0]
    quarter = glob_v.shape[1]
    half = chunk // 2
    count = rows // chunk
    rep = lax.axis_index("rep")
    shard = lax.axis_index("fsdp")
    y, x = rep // 2, rep % 2
    x_peer, y_peer = y * 2 + (1 - x), (1 - y) * 2 + x

    def whole(c):
        return pl.ds(pl.multiple_of(c * chunk, chunk), chunk)

    def first(c):
        return pl.ds(pl.multiple_of(c * chunk, half), half)

    def second(c):
        return pl.ds(pl.multiple_of(c * chunk + half, half), half)

    def packed(c):
        return pl.ds(pl.multiple_of(c * half, half), half)

    def remote(src, dst, kind, c, peer):
        return pltpu.make_async_remote_copy(
            src_ref=src, dst_ref=dst, send_sem=send_sem.at[kind, c], recv_sem=recv_sem.at[kind, c],
            device_id=(peer, shard), device_id_type=MESH,
        )

    def scatter_x(c):
        return remote(pseudo.at[:, 1 - x, first(c)], ra.at[:, packed(c)], 0, c, x_peer)

    def scatter_y(c):
        return remote(pseudo.at[1 - y, :, second(c)], rb.at[:, packed(c)], 1, c, y_peer)

    def pass_y(c):
        return remote(sa.at[packed(c)], r2a.at[packed(c)], 2, c, y_peer)

    def pass_x(c):
        return remote(sb.at[packed(c)], r2b.at[packed(c)], 3, c, x_peer)

    def own_x(c, at_x):
        block = gbf.at[y, at_x, whole(c)]
        return remote(block, block, 4, c, x_peer)

    def own_y(c, at_y):
        block = gbf.at[at_y, x, whole(c)]
        return remote(block, block, 5, c, y_peer)

    def onward_x(c, at_x):
        block = gbf.at[1 - y, at_x, first(c)]
        return remote(block, block, 6, c, x_peer)

    def onward_y(c, at_y):
        block = gbf.at[at_y, 1 - x, second(c)]
        return remote(block, block, 7, c, y_peer)

    def sum_copy(step):
        return pltpu.make_async_remote_copy(
            src_ref=sums.at[0], dst_ref=sums.at[step],
            send_sem=sum_send.at[step - 1], recv_sem=sum_recv.at[step - 1],
            device_id=(rep, (shard + step) % shards), device_id_type=MESH,
        )

    def code_copy(c):
        return pltpu.make_async_copy(
            codes.at[whole(c)], code_v.at[c % SLOTS], code_sem.at[c % SLOTS]
        )

    def inner_copy(c):
        return pltpu.make_async_copy(inner.at[whole(c)], inner_v.at[c % 2], inner_sem.at[c % 2])

    scale_load = pltpu.make_async_copy(scales, scale_v, load_sem.at[0])
    gate_load = pltpu.make_async_copy(gate, gate_v, load_sem.at[1])
    up_load = pltpu.make_async_copy(up, up_v, load_sem.at[2])
    og_load = pltpu.make_async_copy(og, og_v, load_sem.at[3])
    glob_load = pltpu.make_async_copy(glob, glob_v, load_sem.at[4])
    mom_load = pltpu.make_async_copy(mom, mom_v, load_sem.at[5])
    code_copy(0).start()
    scale_load.start()
    for c in range(1, min(SLOTS, count)):
        code_copy(c).start()

    barrier = pltpu.get_barrier_semaphore()

    def signal(semaphore, peer, at_shard):
        pl.semaphore_signal(semaphore, inc=1, device_id=(peer, at_shard), device_id_type=MESH)

    @pl.when(rep == 0)
    def _():
        for peer in (1, 2, 3):
            signal(barrier, peer, shard)

    @pl.when(rep == 3)
    def _():
        for peer in (1, 2):
            signal(barrier, peer, shard)

    def enter():
        @pl.when((rep == 1) | (rep == 2))
        def _():
            pl.semaphore_wait(barrier, 2)
            for peer in (0, 3):
                signal(ready, peer, shard)

        @pl.when(rep == 3)
        def _():
            pl.semaphore_wait(barrier, 1)
            signal(ready, 0, shard)
            pl.semaphore_wait(ready, 2)

        @pl.when(rep == 0)
        def _():
            pl.semaphore_wait(ready, 3)
            for step in range(1, shards):
                signal(barrier, 0, (shard + step) % shards)

    def enter_shards():
        @pl.when(rep == 0)
        def _():
            pl.semaphore_wait(barrier, shards - 1)
            for peer in (1, 2, 3):
                signal(opened, peer, shard)

        @pl.when(rep > 0)
        def _():
            pl.semaphore_wait(opened, 1)

    k = lax.broadcasted_iota(jnp.int32, (256, 256), 0)
    n = lax.broadcasted_iota(jnp.int32, (256, 256), 1)
    j, odd = n >> 1, n & 1
    from_word = jnp.where((k == j) & (odd == 0), 1.0, 0.0)
    from_upper = jnp.where(k == j + 128, jnp.where(odd == 0, -16.0, 1.0), 0.0)
    spread[...] = (from_word + from_upper).astype(jnp.bfloat16)
    squares[...] = jnp.zeros_like(squares)

    def unpack_chunk(c):
        code_copy(c).wait()
        block_scale = scale_v[:, whole(c)].T
        slot = c % SLOTS
        for b in range(code_v.shape[2] // 128):
            word = code_v[slot, :, 128 * b : 128 * b + 128]
            pair = jnp.concatenate(
                [
                    (word - 136).astype(jnp.float32).astype(jnp.bfloat16),
                    ((word >> 4) - 8).astype(jnp.float32).astype(jnp.bfloat16),
                ],
                axis=1,
            )
            centered = jnp.dot(pair, spread[...], preferred_element_type=jnp.float32)
            for part in range(2):
                col = 256 * b + 128 * part
                q, at = col // quarter, col % quarter
                value = centered[:, 128 * part : 128 * part + 128]
                value = value * block_scale[:, 2 * b + part : 2 * b + part + 1]
                pseudo[q // 2, q % 2, whole(c), at : at + 128] = value.astype(jnp.bfloat16)

        @pl.when(c + SLOTS < count)
        def _():
            code_copy(c + SLOTS).start()

    def square_chunk(c):
        wide = 2 * chunk
        cols = pl.ds(pl.multiple_of(c * wide, wide), wide)
        g = gate_v[:, cols].astype(jnp.float32)
        h = g * jax.nn.sigmoid(g) * up_v[:, cols].astype(jnp.float32)
        hid_t[cols, :] = h.T.astype(jnp.bfloat16)
        for q in range(4):
            grad = jnp.dot(
                hid_t[cols, :], og_v[:, quarter * q : quarter * (q + 1)],
                preferred_element_type=jnp.float32,
            ) * (1.0 / tok_total)
            squares[...] += jnp.sum((grad * grad).reshape(wide // 8, 8, quarter), axis=0)

    def send_sums():
        enter_shards()
        sums[0] = jnp.full((8, 128), jnp.sum(squares[...]), jnp.float32)
        for step in range(1, shards):
            sum_copy(step).start()

    def pass_chunk(c):
        scatter_x(c).wait_recv()
        mine = pseudo[1 - y, x, first(c)].astype(jnp.float32)
        sa[packed(c)] = (mine + ra[1 - y, packed(c)].astype(jnp.float32)).astype(jnp.bfloat16)
        pass_y(c).start()
        scatter_y(c).wait_recv()
        mine = pseudo[y, 1 - x, second(c)].astype(jnp.float32)
        sb[packed(c)] = (mine + rb[1 - x, packed(c)].astype(jnp.float32)).astype(jnp.bfloat16)
        pass_x(c).start()

    def outer_rows(at, total):
        new_momentum, new_global = outer_update(total * 0.25, mom_v[at], glob_v[at])
        mom_v[at] = new_momentum
        glob_v[at] = new_global
        gbf[y, x, at] = new_global.astype(jnp.bfloat16)

    def outer_chunk(c):
        f32 = jnp.float32
        pass_y(c).wait_recv()
        at, near = first(c), packed(c)
        outer_rows(at, pseudo[y, x, at].astype(f32) + ra[y, near].astype(f32) + r2a[near].astype(f32))
        pass_x(c).wait_recv()
        at = second(c)
        outer_rows(at, pseudo[y, x, at].astype(f32) + rb[x, near].astype(f32) + r2b[near].astype(f32))
        own_x(c, x).start()
        own_y(c, y).start()

    def find_factor():
        for step in range(1, shards):
            sum_copy(step).wait_recv()
        total = sums[0]
        for step in range(1, shards):
            total = total + sums[step]
        root_mean = jnp.sqrt(total / all_entries + 1e-06)
        scale = jnp.minimum(1.0, 0.02 / root_mean) * (0.4 / tok_total)
        factor[...] = jnp.concatenate([scale] * (quarter // 128), axis=1)

    def onward_chunk(c):
        own_y(c, 1 - y).wait_recv()
        onward_x(c, x).start()
        own_x(c, 1 - x).wait_recv()
        onward_y(c, y).start()

    def merge_chunk(c):
        slot = c % 2
        inner_copy(c).wait()

        for q in range(4):
            cols = slice(quarter * q, quarter * (q + 1))
            grad = jnp.dot(hid_t[whole(c), :], og_v[:, cols], preferred_element_type=jnp.float32)
            kept = 0.42 * inner_v[slot, :, cols].astype(jnp.float32)
            base[:, cols] = kept - grad * factor[0:1, :]

        @pl.when(c + 2 < count)
        def _():
            inner_copy(c + 2).start()

        scatter_x(c).wait_send()
        scatter_y(c).wait_send()
        onward_x(c, 1 - x).wait_recv()
        onward_y(c, 1 - y).wait_recv()
        for q in range(4):
            arrived = gbf[q // 2, q % 2, whole(c)].astype(jnp.float32)
            kept = base[:, quarter * q : quarter * (q + 1)] + 0.5 * arrived
            pseudo[q // 2, q % 2, whole(c)] = kept.astype(jnp.bfloat16)

    enter()
    scale_load.wait()
    unpack_chunk(0)
    for load in (gate_load, up_load, og_load, glob_load, mom_load):
        load.start()
    for c in range(min(2, count)):
        inner_copy(c).start()

    merge_lag = max(4 * LAG, LAG + count // 2)

    def step(s, carry):
        @pl.when(s < count)
        def _():
            scatter_x(s).start()
            scatter_y(s).start()

        @pl.when(s + 1 < count)
        def _():
            unpack_chunk(s + 1)

        @pl.when((s >= LAG) & (s < count + LAG))
        def _():
            pass_chunk(s - LAG)

        @pl.when(s == 2 * LAG)
        def _():
            glob_load.wait()
            mom_load.wait()

        @pl.when((s >= 2 * LAG) & (s < count + 2 * LAG))
        def _():
            outer_chunk(s - 2 * LAG)

        @pl.when((s >= 3 * LAG) & (s < count + 3 * LAG))
        def _():
            onward_chunk(s - 3 * LAG)

        @pl.when(s == LAG)
        def _():
            gate_load.wait()
            up_load.wait()
            og_load.wait()

        @pl.when((s >= LAG) & (s < LAG + count // 2))
        def _():
            square_chunk(s - LAG)

        @pl.when(s == LAG + count // 2 - 1)
        def _():
            send_sums()

        @pl.when(s == merge_lag)
        def _():
            find_factor()

        @pl.when(s >= merge_lag)
        def _():
            merge_chunk(s - merge_lag)

        return carry

    lax.fori_loop(0, count + merge_lag, step, 0)

    def drain(c, carry):
        pass_y(c).wait_send()
        pass_x(c).wait_send()
        own_x(c, x).wait_send()
        own_y(c, y).wait_send()
        onward_x(c, x).wait_send()
        onward_y(c, y).wait_send()
        return carry

    lax.fori_loop(0, count, drain, 0)
    for step in range(1, shards):
        sum_copy(step).wait_send()


def write_results(merged_v, glob_v, mom_v, merged_out, glob_out, mom_out, sem):
    rows, quarter = glob_v.shape
    copies = []
    for q in range(4):
        place = merged_out.at[:, pl.ds(quarter * q, quarter)]
        copies.append(pltpu.make_async_copy(merged_v.at[q // 2, q % 2], place, sem.at[q]))
    for index, (held, out) in enumerate(((glob_v, glob_out), (mom_v, mom_out))):
        for part in range(2):
            at = pl.ds(part * (rows // 2), rows // 2)
            copies.append(
                pltpu.make_async_copy(held.at[at], out.at[at], sem.at[4 + 2 * index + part])
            )
    for copy in copies:
        copy.start()
    for copy in copies:
        copy.wait()


def per_device_square(
    gate_pre, up_pre, out_grad, inner_params, global_params, outer_momentum, pair_codes, code_scales
):
    shards = lax.axis_size("fsdp")
    tokens, rows = gate_pre.shape
    width = out_grad.shape[1]
    quarter = width // 4
    chunk = 128
    count = rows // chunk
    bf16, f32 = jnp.bfloat16, jnp.float32
    dma = pltpu.SemaphoreType.DMA
    any_spec = pl.BlockSpec(memory_space=pl.ANY)
    vmem_spec = pl.BlockSpec(memory_space=pltpu.VMEM)
    merged, new_global, new_momentum = pl.pallas_call(
        functools.partial(fused_step, chunk, shards, tokens, rows * shards * width),
        out_shape=(
            pltpu.VMEM((2, 2, rows, quarter), bf16),
            pltpu.VMEM((rows, quarter), f32),
            pltpu.VMEM((rows, quarter), f32),
        ),
        in_specs=[any_spec] * 8,
        out_specs=(vmem_spec,) * 3,
        scratch_shapes=[
            pltpu.VMEM((2, rows // 2, quarter), bf16),
            pltpu.VMEM((2, rows // 2, quarter), bf16),
            pltpu.VMEM((rows // 2, quarter), bf16),
            pltpu.VMEM((rows // 2, quarter), bf16),
            pltpu.VMEM((rows // 2, quarter), bf16),
            pltpu.VMEM((rows // 2, quarter), bf16),
            pltpu.VMEM((2, 2, rows, quarter), bf16),
            pltpu.VMEM((SLOTS, chunk, width // 2), jnp.int32),
            pltpu.VMEM((code_scales.shape[2], rows), f32),
            pltpu.VMEM((tokens, rows), bf16),
            pltpu.VMEM((tokens, rows), bf16),
            pltpu.VMEM((tokens, width), bf16),
            pltpu.VMEM((rows, tokens), bf16),
            pltpu.VMEM((2, chunk, width), bf16),
            pltpu.VMEM((chunk, width), f32),
            pltpu.VMEM((256, 256), bf16),
            pltpu.VMEM((8, quarter), f32),
            pltpu.VMEM((shards, 8, 128), f32),
            pltpu.VMEM((8, quarter), f32),
            dma((8, count)),
            dma((8, count)),
            dma((shards - 1,)),
            dma((shards - 1,)),
            dma((SLOTS,)),
            dma((6,)),
            dma((2,)),
            pltpu.SemaphoreType.REGULAR,
            pltpu.SemaphoreType.REGULAR,
        ],
        compiler_params=pltpu.CompilerParams(
            collective_id=0, has_side_effects=True, vmem_limit_bytes=40 * 1024 * 1024
        ),
        cost_estimate=pl.CostEstimate(
            flops=4 * tokens * rows * width, bytes_accessed=22 * rows * width, transcendentals=0
        ),
    )(
        gate_pre, up_pre, out_grad, inner_params[0], global_params, outer_momentum,
        pair_codes[0], code_scales[0].T,
    )
    merged, new_global, new_momentum = pl.pallas_call(
        write_results,
        out_shape=(
            jax.ShapeDtypeStruct((rows, width), bf16),
            jax.ShapeDtypeStruct((rows, quarter), f32),
            jax.ShapeDtypeStruct((rows, quarter), f32),
        ),
        in_specs=[vmem_spec] * 3,
        out_specs=(any_spec,) * 3,
        scratch_shapes=[dma((8,))],
        compiler_params=pltpu.CompilerParams(vmem_limit_bytes=4 * 1024 * 1024),
        cost_estimate=pl.CostEstimate(
            flops=0, bytes_accessed=4 * rows * width, transcendentals=0
        ),
    )(merged, new_global, new_momentum)
    return (merged[None], new_global, new_momentum)


def per_device(*arrays):
    rows, width = arrays[0].shape[1], arrays[2].shape[1]
    square = lax.axis_size("rep") == 4 and lax.axis_size("fsdp") > 1
    if square and rows % 256 == 0 and width % 1024 == 0 and width // arrays[7].shape[2] == 128:
        return per_device_square(*arrays)
    return per_device_any(*arrays)


def solution(mesh):
    in_specs = (
        P("rep", "fsdp"),
        P("rep", "fsdp"),
        P("rep", None),
        P("rep", "fsdp", None),
        P("fsdp", "rep"),
        P("fsdp", "rep"),
        P("rep", "fsdp", None),
        P("rep", "fsdp", None),
    )
    out_specs = (P("rep", "fsdp", None), P("fsdp", "rep"), P("fsdp", "rep"))
    return jax.shard_map(
        per_device, mesh=mesh, in_specs=in_specs, out_specs=out_specs, check_vma=False
    )
```
